256 devices in a mesh: feat: 4 (over y), dom: 64 (over x, z, core).
Axes of the slice: x: 4, y: 4, z: 8, core: 2. Of those that a mesh axis runs over, the one named last changes fastest.
Arguments:
- feats: bfloat16 [32768, 128], P('dom', 'feat'), may hold values from -6 to 6
- tile_src: int32 [16384], P('dom'), may hold values from 0 to 3
- tile_dst: int32 [16384], P('dom'), may hold values from 0 to 255
- tile_val: bfloat16 [16384, 128, 128], P('dom'), may hold values from 0 to 0.125, as said below
- tile_count: int32 [64], P('dom'), may hold values from 64 to 256, as said below
- self_one: bfloat16 [128, 256], P('feat'), may hold values from -0.5 to 0.5
- neigh_one: bfloat16 [128, 256], P('feat'), may hold values from -0.5 to 0.5
- bias_one: float32 [256], P('feat'), may hold values from -3 to 3
- self_two: bfloat16 [256, 256], P('feat'), may hold values from -0.375 to 0.375
- neigh_two: bfloat16 [256, 256], P('feat'), may hold values from -0.375 to 0.375
- bias_two: float32 [256], P('feat'), may hold values from -3 to 3
Outputs:
- hidden_two: bfloat16 [32768, 256], P('dom', 'feat')
The draws below stay inside these ranges and needn't reach their ends.
Inputs may be any that keep to these rules, and one draw needn't show every extreme that they name: `tile_count`: partitions hold differing numbers of live tiles; some partition has all 256 slots live in every draw. `tile_val`: most entries are zero.
All inputs are finite; a program needn't handle non-finite values.
Results may differ from the reference program's by a relative error of at most 0.0034.
Values sent between devices are 32-bit elements; how exact they have to be, the bound alone decides.
A program may use at most 128 MiB of HBM per device.

```python
import jax
import jax.numpy as jnp
from jax import lax

F = 128
H = 256
BLK = 128
NB_DEV = 4
TILES = 256
NODES = 32768
NBLK = 256
N_DOM = 64


def draw_tile_count(key, part):
    key = jax.random.fold_in(key, 7)
    first, second = jax.random.split(key)
    counts = jax.random.randint(first, (N_DOM,), max(1, TILES // 4), TILES + 1)
    fullest = jax.random.randint(second, (), 0, N_DOM)
    return jnp.where(jnp.arange(N_DOM) == fullest, TILES, counts).astype(jnp.int32)


def draw_tile_val(key, part):
    key = jax.random.fold_in(key, 11)
    chance = jax.random.uniform(key, (TILES * N_DOM, BLK, BLK), jnp.float32)
    scaled = chance * 64.0
    level = 0.125 * (1.0 - scaled)
    return jnp.where(scaled < 1.0, level, 0.0).astype(jnp.float32).astype(jnp.bfloat16)


def plant(values, own_key, smallest, largest):
    place = [jax.random.randint(jax.random.fold_in(own_key, axis), (), 0, length) for axis, length in enumerate(values.shape)]
    widest = values.shape.index(max(values.shape))
    next_to = place[:widest] + [(place[widest] + 1) % values.shape[widest]] + place[widest + 1:]
    return values.at[tuple(place)].set(smallest).at[tuple(next_to)].set(largest)


def level_of(own_key, dims, cuts, smallest, high):
    loudness = 1.0
    for dim, shards_of in cuts:
        heights = jax.random.uniform(jax.random.fold_in(jax.random.fold_in(own_key, 6), dim), (shards_of,), jnp.float32, smallest / len(cuts), high / len(cuts))
        loudness = loudness * jnp.repeat(jnp.exp(heights), dims[dim] // shards_of).reshape((-1,) + (1,) * (len(dims) - 1 - dim))
    return loudness


def scatter_about(own_key, extent, deviation, limit, cuts=(), kind=jnp.bfloat16):
    loudness = level_of(own_key, extent, cuts, -0.22, 0.18) if cuts else 1.0
    entries = jax.random.normal(own_key, extent, jnp.float32) * deviation * loudness
    return jnp.minimum(jnp.maximum(entries, -limit), limit).astype(kind)


def setup_inputs(seed: int = 0) -> dict:
    keys = jax.random.split(jax.random.key(seed), 12)
    feats = scatter_about(keys[0], (NODES, F), 1.0, 6.0, ((0, 64), (1, 4)))
    tile_src = plant(jax.random.randint(keys[1], (TILES * N_DOM,), 0, NB_DEV), jax.random.fold_in(keys[1], 1), 0, NB_DEV - 1).astype(jnp.int32)
    tile_dst = plant(jax.random.randint(keys[2], (TILES * N_DOM,), 0, NBLK), jax.random.fold_in(keys[2], 1), 0, NBLK - 1).astype(jnp.int32)
    tile_val = draw_tile_val(jax.random.fold_in(keys[11], 71), 0)
    tile_count = draw_tile_count(jax.random.fold_in(keys[11], 71), 0)
    self_one = scatter_about(keys[5], (F, H), F ** -0.5, 0.5, ((0, 4),))
    neigh_one = scatter_about(keys[6], (F, H), F ** -0.5, 0.5, ((0, 4),))
    bias_one = scatter_about(keys[7], (H,), 0.5, 3.0, ((0, 4),), jnp.float32)
    self_two = scatter_about(keys[8], (H, H), H ** -0.5, 0.375, ((0, 4),))
    neigh_two = scatter_about(keys[9], (H, H), H ** -0.5, 0.375, ((0, 4),))
    bias_two = scatter_about(keys[10], (H,), 0.5, 3.0, ((0, 4),), jnp.float32)
    return dict(feats=feats, tile_src=tile_src, tile_dst=tile_dst, tile_val=tile_val, tile_count=tile_count, self_one=self_one, neigh_one=neigh_one, bias_one=bias_one, self_two=self_two, neigh_two=neigh_two, bias_two=bias_two)


def aggregate(values, tile_src, tile_dst, tile_val, tile_count):
    width = values.shape[1]
    blocked = values.reshape(N_DOM, NB_DEV, BLK, width)
    sources = tile_src.reshape(N_DOM, TILES)
    targets = tile_dst.reshape(N_DOM, TILES)
    weights = tile_val.reshape(N_DOM, TILES, BLK, BLK)

    def step(carry, inputs):
        blocks_here, source, target, weight, count = inputs
        picked = blocks_here[source].astype(jnp.float32)
        messages = jnp.einsum("tij,tjc->tic", weight.astype(jnp.float32), picked)
        live = jnp.arange(TILES) < count
        messages = jnp.where(live[:, None, None], messages, jnp.zeros_like(messages))
        return carry.at[target].add(messages), None

    start = jnp.zeros((NB_DEV * N_DOM, BLK, width), jnp.float32)
    total, unused = lax.scan(step, start, (blocked, sources, targets, weights, tile_count))
    return total.reshape(NB_DEV * N_DOM * BLK, width)


def reference(feats, tile_src, tile_dst, tile_val, tile_count, self_one, neigh_one, bias_one, self_two, neigh_two, bias_two):
    highest = lax.Precision.HIGHEST
    agg_one = aggregate(feats, tile_src, tile_dst, tile_val, tile_count)
    pre_one = jnp.dot(feats, self_one, preferred_element_type=jnp.float32)
    pre_one = pre_one + jnp.dot(agg_one, neigh_one.astype(jnp.float32), precision=highest) + bias_one
    hidden_one = jnp.maximum(pre_one, 0.0).astype(jnp.bfloat16)
    agg_two = aggregate(hidden_one, tile_src, tile_dst, tile_val, tile_count)
    pre_two = jnp.dot(hidden_one, self_two, preferred_element_type=jnp.float32)
    pre_two = pre_two + jnp.dot(agg_two, neigh_two.astype(jnp.float32), precision=highest) + bias_two
    return jnp.maximum(pre_two, 0.0).astype(jnp.bfloat16)
```

```python
import functools

import jax
import jax.numpy as jnp
from jax import lax
from jax.experimental import pallas as pl
from jax.experimental.pallas import tpu as pltpu
from jax.sharding import PartitionSpec as P

MESH = pl.DeviceIdType.MESH
BLK = 128
QUARTER = 32
XS, ZS, FS = 4, 8, 4
TILES = 256
GROUP = 32
PACK_ROWS = 200
F32, BF16 = jnp.float32, jnp.bfloat16


def position():
    dom = lax.axis_index("dom")
    return lax.div(dom, 2 * ZS), lax.rem(lax.div(dom, 2), ZS), lax.rem(dom, 2)


def rank_of(offset, middle):
    return 2 * (offset - middle) if offset >= middle else 2 * (middle - offset) - 1


def chunk_x(dx, half):
    return 2 * (2 * rank_of(dx, XS // 2) + half) + 1


def chunk_z(dz):
    return 2 * rank_of(dz, ZS // 2)


def traced_rank(offset, middle):
    ahead = offset - middle
    return jnp.where(ahead >= 0, 2 * ahead, -2 * ahead - 1)


def build_kernel(
    count_ref, src_ref, dst_ref, tiles_ref, feats_ref, self_one_ref, neigh_one_ref, bias_one_ref, self_two_ref,
    neigh_two_ref, bias_two_ref, adj, feats_out, pack_out,
    tiles, src, dst, feats, self_one, neigh_one, bias_one, self_two, neigh_two, bias_two, total, order, cells, earlier,
    last, in_sems, small_sems,
):
    def load(source, target, n):
        copy = pltpu.make_async_copy(source, target, small_sems.at[n])
        copy.start()
        return copy

    index_loads = [load(src_ref, src, 0), load(dst_ref, dst, 1)]
    loads = []
    groups = TILES // GROUP
    for g in range(groups):
        part = pl.ds(g * GROUP, GROUP)
        loads.append(pltpu.make_async_copy(tiles_ref.at[part], tiles.at[part], in_sems.at[g]))
        loads[-1].start()
    weight_loads = [
        load(feats_ref, feats, 2), load(self_one_ref, self_one, 3), load(neigh_one_ref, neigh_one, 4),
        load(bias_one_ref, bias_one, 5), load(self_two_ref, self_two, 6), load(neigh_two_ref, neigh_two, 7),
        load(bias_two_ref, bias_two, 8),
    ]
    feat = lax.axis_index("feat")
    x, z, core = position()
    count = count_ref[0]

    def clear(i, carry):
        adj[i] = jnp.zeros(adj.shape[1:], BF16)
        return carry

    lax.fori_loop(0, adj.shape[0], clear, 0)

    def forget(i, carry):
        last[i] = -1
        return carry

    lax.fori_loop(0, 256, forget, 0, unroll=16)
    for copy in index_loads:
        copy.wait()

    def look(t, hits):
        to = dst[t]
        dom = lax.shift_right_logical(to, 2)
        other = lax.bitwise_xor(dom & 1, core)
        dz = (lax.shift_right_logical(dom, 1) - z) & (ZS - 1)
        dx = (lax.shift_right_logical(dom, 4) - x) & (XS - 1)
        mine = jnp.logical_and((to & 3) == feat, t < count)
        cell = jnp.where(mine, ((other * XS + dx) * ZS + dz) * 4 + src[t], 256)
        earlier[t] = last[cell]
        last[cell] = t
        order[hits] = t
        cells[hits] = cell
        return hits + mine.astype(jnp.int32)

    ends = [jnp.int32(0)]
    for g in range(groups):
        ends.append(lax.fori_loop(g * GROUP, (g + 1) * GROUP, look, ends[-1], unroll=8))

    for copy in weight_loads:
        copy.wait()
    feats_out[...] = feats[...].astype(F32)
    pack_out[0:32, :] = self_one[...].astype(F32)
    pack_out[32:64, :] = neigh_one[...].astype(F32)
    pack_out[64:128, :] = self_two[...].astype(F32)
    pack_out[128:192, :] = neigh_two[...].astype(F32)
    pack_out[192:200, :] = jnp.zeros((8, 256), F32)
    pack_out[192:193, 0:64] = bias_one[...]
    pack_out[193:194, 0:64] = bias_two[...]

    def put(cell, value):
        source = cell & 3
        dz = lax.shift_right_logical(cell, 2) & (ZS - 1)
        dx = lax.shift_right_logical(cell, 5) & (XS - 1)
        base = lax.shift_right_logical(cell, 7) * 16
        lanes = pl.ds(pl.multiple_of(source * BLK, BLK), BLK)
        rank_x, rank_z = traced_rank(dx, XS // 2), traced_rank(dz, ZS // 2)
        for half in range(2):
            chunk = base + 2 * (2 * rank_x + half) + 1
            rows = pl.ds(pl.multiple_of(rank_z * QUARTER, QUARTER), QUARTER)
            adj[chunk, rows, lanes] = value[half * QUARTER : (half + 1) * QUARTER]
        chunk = base + 2 * rank_z
        for half in range(2):
            rows = pl.ds(pl.multiple_of(half * BLK + rank_x * QUARTER, QUARTER), QUARTER)
            adj[chunk, rows, lanes] = value[64 + half * QUARTER : 64 + (half + 1) * QUARTER]

    def fill(i, carry):
        t = order[i]
        cell = cells[i]
        before = earlier[t]

        @pl.when(last[cell] == t)
        def _():
            @pl.when(before < 0)
            def _():
                put(cell, tiles[t])

            @pl.when(before >= 0)
            def _():
                total[...] = tiles[t].astype(F32)

                def more(at):
                    total[...] += tiles[at].astype(F32)
                    return earlier[at]

                lax.while_loop(lambda at: at >= 0, more, before)
                put(cell, total[...].astype(BF16))

        return carry

    for g in range(groups):
        loads[g].wait()
        lax.fori_loop(ends[g], ends[g + 1], fill, 0)


def build(src, dst, count, tiles, feats, self_one, neigh_one, bias_one, self_two, neigh_two, bias_two):
    vmem = pl.BlockSpec(memory_space=pltpu.VMEM)
    hbm = pl.BlockSpec(memory_space=pltpu.HBM)
    arrays = [src, dst, tiles, feats, self_one, neigh_one, bias_one, self_two, neigh_two, bias_two]
    arrays = [pltpu.with_memory_space_constraint(array, pltpu.HBM) for array in arrays]
    smem = [pltpu.SMEM((TILES + 8,), jnp.int32)] * 3 + [pltpu.SMEM((264,), jnp.int32)]
    return pl.pallas_call(
        build_kernel,
        out_shape=(
            pltpu.VMEM((32, 256, 512), BF16),
            pltpu.VMEM((32, 512), F32),
            pltpu.VMEM((PACK_ROWS, 256), F32),
        ),
        in_specs=[pl.BlockSpec(memory_space=pltpu.SMEM)] + [hbm] * 10,
        out_specs=(vmem, vmem, vmem),
        scratch_shapes=[
            pltpu.VMEM((TILES, BLK, BLK), BF16),
            pltpu.SMEM((TILES,), jnp.int32),
            pltpu.SMEM((TILES,), jnp.int32),
        ]
        + [pltpu.VMEM(array.shape, array.dtype) for array in arrays[3:]]
        + [pltpu.VMEM((BLK, BLK), F32)]
        + smem
        + [pltpu.SemaphoreType.DMA((TILES // GROUP,)), pltpu.SemaphoreType.DMA((9,))],
        compiler_params=pltpu.CompilerParams(vmem_limit_bytes=12 << 20),
    )(count, *arrays)


def add_up(into, terms):
    rows = into.shape[0]
    step = rows if rows <= 160 else BLK

    def body(i, carry):
        part = pl.ds(pl.multiple_of(i * step, step), step)
        value = terms[0][part, :]
        for term in terms[1:]:
            value = value + term[part, :]
        into[part, :] = value
        return carry

    if rows == step:
        body(0, 0)
    else:
        lax.fori_loop(0, rows // step, body, 0)


class Ring:
    def __init__(self, n, own, extra, land, up_id, down_id, sends, recvs, started):
        self.n, self.middle = n, n // 2
        self.own, self.extra, self.land = own, extra, land
        self.ids = (up_id, down_id)
        self.sends, self.recvs, self.started = sends, recvs, started

    def copy(self, way, distance, half):
        offset = distance if way == 0 else self.n - distance
        slot = (way * self.middle + distance - 1) * 2 + half
        return pltpu.make_async_remote_copy(
            src_ref=self.own(offset, half),
            dst_ref=self.land(way, distance - 1, half),
            send_sem=self.sends.at[slot],
            recv_sem=self.recvs.at[slot],
            device_id=self.ids[way],
            device_id_type=MESH,
        )

    def gather_terms(self, way, distance, half):
        first = self.middle if way == half else self.middle - 1
        if distance == first:
            return []
        self.copy(way, distance + 1, half).wait_recv()
        return [self.land(way, distance, half)]

    def send(self, way, distance, half):
        offset = distance if way == 0 else self.n - distance
        mine = self.own(offset, half)
        terms = [mine] + self.extra(offset, half) + self.gather_terms(way, distance, half)
        if len(terms) > 1:
            add_up(mine, terms)
        copy = self.copy(way, distance, half)
        copy.start()
        self.started.append(copy)

    def early(self, distance):
        self.send(0, distance, 1)
        self.send(1, distance, 0)

    def late(self, distance):
        self.send(0, distance, 0)
        self.send(1, distance, 1)

    def finish(self, half, into=None):
        mine = self.own(0, half)
        terms = [mine] + self.extra(0, half)
        for way in range(2):
            terms += self.gather_terms(way, 0, half)
        add_up(mine if into is None else into, terms)


def split(value):
    high = value.astype(BF16)
    rest = value - high.astype(F32)
    middle = rest.astype(BF16)
    low = (rest - middle.astype(F32)).astype(BF16)
    return high, middle, low


def dot(a, b):
    return jnp.dot(a, b, preferred_element_type=F32)


Z_GROUPS = ((0, 96), (96, 32))
X_GROUPS = ((0, 160), (160, 96))
TOGETHER = 2


def reduce_scatter(adj, rhs, bufs, sems, ids, started, before_end, on_z_rows, on_x_rows):
    sums, sent, got, z_up, z_down, x_up, x_down, tz_up, tz_down, tx_up, tx_down = bufs
    pair_sends, pair_recvs, sends, recvs = sems
    pair_id, zp_id, zm_id, xp_id, xm_id = ids
    width = rhs.shape[1]

    def pair_copy(chunk):
        return pltpu.make_async_remote_copy(
            src_ref=sent.at[chunk], dst_ref=got.at[chunk], send_sem=pair_sends.at[chunk],
            recv_sem=pair_recvs.at[chunk], device_id=pair_id, device_id_type=MESH,
        )

    def product(first, target, at):
        lhs = adj[pl.ds(first, TOGETHER)].reshape(TOGETHER * 256, 512)
        target[pl.ds(at, TOGETHER)] = dot(lhs, rhs[...]).reshape(TOGETHER, 256, width)

    def for_pair(i, carry):
        product(16 + i * TOGETHER, sent, i * TOGETHER)
        for k in range(TOGETHER):
            pair_copy(i * TOGETHER + k).start()
        return carry

    def for_own(i, carry):
        product(i * TOGETHER, sums, i * TOGETHER)
        return carry

    def run(kind, first, end):
        lax.fori_loop(first // TOGETHER, end // TOGETHER, kind, 0)

    have = set()

    def arrived(chunk):
        if chunk not in have:
            have.add(chunk)
            pair_copy(chunk).wait_recv()

    def none(offset, half):
        return []

    def z_part(group):
        first, size = Z_GROUPS[group]

        def own(dz, half):
            return sums.at[chunk_z(dz), pl.ds(half * BLK + first, size)]

        def extra(dz, half):
            arrived(chunk_z(dz))
            return [got.at[chunk_z(dz), pl.ds(half * BLK + first, size)]]

        def land(way, at, half):
            return (z_up, z_down)[way].at[at, half, pl.ds(first, size)]

        slots = pl.ds(group * 16, 16)
        return Ring(ZS, own, extra, land, zp_id, zm_id, sends.at[slots], recvs.at[slots], started)

    def x_part(group):
        first, size = X_GROUPS[group]

        def own(dx, half):
            return sums.at[chunk_x(dx, half), pl.ds(first, size)]

        def extra(dx, half):
            arrived(chunk_x(dx, half))
            return [got.at[chunk_x(dx, half), pl.ds(first, size)]]

        def land(way, at, half):
            return (x_up, x_down)[way].at[at, half, pl.ds(first, size)]

        slots = pl.ds(32 + group * 8, 8)
        return Ring(XS, own, extra, land, xp_id, xm_id, sends.at[slots], recvs.at[slots], started)

    def last_z():
        def own(dz, half):
            return sums.at[chunk_x(0, half), pl.ds(rank_of(dz, ZS // 2) * QUARTER, QUARTER)]

        def land(way, at, half):
            return (tz_up, tz_down)[way].at[at, half]

        slots = pl.ds(48, 16)
        return Ring(ZS, own, none, land, zp_id, zm_id, sends.at[slots], recvs.at[slots], started)

    def last_x():
        def own(dx, half):
            return sums.at[chunk_z(0), pl.ds(half * BLK + rank_of(dx, XS // 2) * QUARTER, QUARTER)]

        def land(way, at, half):
            return (tx_up, tx_down)[way].at[at, half]

        slots = pl.ds(64, 8)
        return Ring(XS, own, none, land, xp_id, xm_id, sends.at[slots], recvs.at[slots], started)

    z0, z1, x0, x1, tz, tx = z_part(0), z_part(1), x_part(0), x_part(1), last_z(), last_x()

    run(for_pair, 0, 4)
    run(for_own, 0, 4)
    run(for_pair, 4, 8)
    z0.late(4)
    x0.late(2)
    run(for_pair, 8, 16)
    run(for_own, 4, 8)
    z0.early(3)
    run(for_own, 8, 12)
    x0.early(1)
    z1.late(4)
    run(for_own, 12, 16)
    z0.late(3)
    z1.early(3)
    x0.late(1)
    x1.late(2)
    x1.early(1)
    z0.early(2)
    z1.late(3)
    z0.late(2)
    z1.early(2)
    z0.early(1)
    x0.finish(0)
    x0.finish(1)
    tz.late(4)
    tz.early(3)
    z0.late(1)
    x1.late(1)
    z1.late(2)
    tz.late(3)
    z1.early(1)
    tz.early(2)
    z0.finish(0)
    z0.finish(1)
    tx.late(2)
    tx.early(1)
    z1.late(1)
    tz.late(2)
    before_end()
    tx.late(1)
    x1.finish(0)
    x1.finish(1)
    tz.early(1)
    tz.late(1)
    z1.finish(0)
    z1.finish(1)
    on_z_rows(tx)
    on_x_rows(tz)

    def drain(chunk, carry):
        pair_copy(chunk).wait_send()
        return carry

    return lambda: lax.fori_loop(0, 16, drain, 0)


def net_kernel(adj, feats_ref, pack_ref, out_ref, *scratch):
    (
        feats_all, packs, feats, hidden, self_one, neigh_one, self_two, neigh_two, bias, own_part, agg_all, agg_two, slices,
        landed, *rest
    ) = scratch
    bufs_one, bufs_two, rest = rest[:11], rest[11:22], rest[22:]
    y_sends, y_recvs, sems_one, sems_two = rest[0], rest[1], rest[2:6], rest[6:10]

    feat = lax.axis_index("feat")
    x, z, core = position()

    def at(x_at, z_at, core_at, feat_at=feat):
        return feat_at, (x_at * ZS + z_at) * 2 + core_at

    pair_id = at(x, z, 1 - core)
    zp_id, zm_id = at(x, lax.rem(z + 1, ZS), core), at(x, lax.rem(z + ZS - 1, ZS), core)
    xp_id, xm_id = at(lax.rem(x + 1, XS), z, core), at(lax.rem(x + XS - 1, XS), z, core)
    y_ids = [at(x, z, core, lax.rem(feat + k, FS)) for k in range(1, FS)]
    ids = (pair_id, zp_id, zm_id, xp_id, xm_id)

    barrier = pltpu.get_barrier_semaphore()
    for other in ids + tuple(y_ids):
        pl.semaphore_signal(barrier, inc=1, device_id=other, device_id_type=MESH)
    pl.semaphore_wait(barrier, 8)

    started = []

    def to_y(kind, source, target):
        copies = []
        for k in range(1, FS):
            slot = kind * 3 + k - 1
            copies.append(
                pltpu.make_async_remote_copy(
                    src_ref=source(k), dst_ref=target, send_sem=y_sends.at[slot], recv_sem=y_recvs.at[slot],
                    device_id=y_ids[k - 1], device_id_type=MESH,
                )
            )
            copies[-1].start()
        started.extend(copies)
        return copies

    def received(copies):
        for copy in copies:
            copy.wait_recv()

    feats_rows = pl.ds(pl.multiple_of(feat * 32, 32), 32)
    feats_copies = to_y(0, lambda k: feats_ref, feats_all.at[feats_rows])
    pack_copies = to_y(1, lambda k: pack_ref, packs.at[feat])
    feats_all[feats_rows, :] = feats_ref[...]
    packs[feat] = pack_ref[...]
    received(feats_copies)
    feats[...] = feats_all[...].T.astype(BF16)

    def take_weights():
        received(pack_copies)
        low = lax.broadcasted_iota(jnp.int32, (1, BLK), 1) < 64
        for row in range(2):
            for pair in range(2):
                left = packs[2 * pair, 192 + row : 193 + row, 0:BLK]
                right = packs[2 * pair + 1, 192 + row : 193 + row, 0:BLK]
                value = jnp.where(low, left, pltpu.roll(right, 64, 1))
                bias[row : row + 1, pair * BLK : (pair + 1) * BLK] = value
        for j in range(FS):
            self_one[32 * j : 32 * (j + 1), :] = packs[j, 0:32, :].astype(BF16)
            neigh_one[32 * j : 32 * (j + 1), :] = packs[j, 32:64, :].astype(BF16)
            self_two[64 * j : 64 * (j + 1), :] = packs[j, 64:128, :].astype(BF16)
            neigh_two[64 * j : 64 * (j + 1), :] = packs[j, 128:192, :].astype(BF16)

        own_part[...] = dot(feats[...], self_one[...]) + bias[0:1, :]

    own = pl.ds(pl.multiple_of(feat * BLK, BLK), BLK)

    def own_of_two():
        own_part[0:BLK, :] = dot(hidden[own, :], self_two[...]) + bias[1:2, :]

    agg_copies = []

    def share(kind, rows, ring):
        for half in range(2):
            ring.finish(half, agg_all.at[feat, pl.ds(rows + half * QUARTER, QUARTER)])
        part = agg_all.at[feat, pl.ds(rows, 64)]
        agg_copies.extend(to_y(kind, lambda k: part, part))

    drain_one = reduce_scatter(
        adj, feats, bufs_one, sems_one, ids, started, take_weights,
        lambda ring: share(2, 64, ring), lambda ring: share(3, 0, ring),
    )
    received(agg_copies)

    def hide(j, carry):
        rows = pl.ds(pl.multiple_of(j * BLK, BLK), BLK)
        pre = own_part[rows, :]
        for part in split(agg_all[j]):
            pre = pre + dot(part, neigh_one[...])
        hidden[rows, :] = jnp.maximum(pre, 0.0).astype(BF16)
        return carry

    lax.fori_loop(0, FS, hide, 0)

    def keep(rows, ring):
        for half in range(2):
            ring.finish(half, agg_two.at[pl.ds(rows + half * QUARTER, QUARTER)])

    drain_two = reduce_scatter(
        adj, hidden, bufs_two, sems_two, ids, started, own_of_two,
        lambda ring: keep(64, ring), lambda ring: keep(0, ring),
    )

    pre = own_part[0:BLK, :]
    for part in split(agg_two[...]):
        pre = pre + dot(part, neigh_two[...])
    result = jnp.maximum(pre, 0.0)
    slices[...] = result.T.reshape(FS, 64, BLK)
    out_copies = to_y(4, lambda k: slices.at[lax.rem(feat + k, FS)], landed.at[feat])
    landed[feat] = slices[feat]
    received(out_copies)
    for j in range(FS):
        out_ref[:, j * BLK : (j + 1) * BLK] = landed[j].astype(BF16)

    drain_one()
    drain_two()
    for copy in started:
        copy.wait_send()


def layer_buffers(width):
    shapes = [(16, 256, width)] * 3
    shapes += [(4, 2, 128, width)] * 2 + [(2, 2, 256, width)] * 2 + [(4, 2, 32, width)] * 2 + [(2, 2, 32, width)] * 2
    return [pltpu.VMEM(shape, F32) for shape in shapes]


def net(adj, feats, pack):
    vmem = pl.BlockSpec(memory_space=pltpu.VMEM)
    dma = pltpu.SemaphoreType.DMA
    return pl.pallas_call(
        net_kernel,
        out_shape=jax.ShapeDtypeStruct((64, 512), BF16),
        in_specs=[vmem] * 3,
        out_specs=vmem,
        scratch_shapes=[
            pltpu.VMEM((128, 512), F32),
            pltpu.VMEM((FS, PACK_ROWS, 256), F32),
            pltpu.VMEM((512, 128), BF16),
            pltpu.VMEM((512, 256), BF16),
            pltpu.VMEM((128, 256), BF16),
            pltpu.VMEM((128, 256), BF16),
            pltpu.VMEM((256, 256), BF16),
            pltpu.VMEM((256, 256), BF16),
            pltpu.VMEM((8, 256), F32),
            pltpu.VMEM((512, 256), F32),
            pltpu.VMEM((FS, 128, 128), F32),
            pltpu.VMEM((128, 256), F32),
            pltpu.VMEM((FS, 64, 128), F32),
            pltpu.VMEM((FS, 64, 128), F32),
        ]
        + layer_buffers(128)
        + layer_buffers(256)
        + [dma((15,)), dma((15,))]
        + [dma((16,)), dma((16,)), dma((72,)), dma((72,))] * 2,
        compiler_params=pltpu.CompilerParams(
            collective_id=0, has_side_effects=True, vmem_limit_bytes=36 << 20
        ),
    )(*[pltpu.with_memory_space_constraint(array, pltpu.VMEM) for array in (adj, feats, pack)])


def on_device(
    feats, tile_src, tile_dst, tile_val, tile_count, self_one, neigh_one, bias_one, self_two, neigh_two, bias_two
):
    adj, columns, pack = build(
        tile_src, tile_dst, tile_count, tile_val, feats.T, self_one, neigh_one, bias_one.reshape(1, 64), self_two,
        neigh_two, bias_two.reshape(1, 64),
    )
    return net(adj, columns, pack).T


def solution(mesh):
    placed = (
        P("dom", "feat"),
        P("dom"),
        P("dom"),
        P("dom", None, None),
        P("dom"),
        P("feat", None),
        P("feat", None),
        P("feat"),
        P("feat", None),
        P("feat", None),
        P("feat"),
    )
    return jax.shard_map(
        on_device, mesh=mesh, in_specs=placed, out_specs=P("dom", "feat"), check_vma=False
    )
```

```python
import functools

import jax
import jax.numpy as jnp
from jax import lax
from jax.experimental import pallas as pl
from jax.experimental.pallas import tpu as pltpu
from jax.sharding import PartitionSpec as P

MESH = pl.DeviceIdType.MESH
BLK = 128
QUARTER = 32
XS, ZS, FS = 4, 8, 4
TILES = 256
GROUP = 32
PACK_ROWS = 200
F32, BF16 = jnp.float32, jnp.bfloat16


def position():
    dom = lax.axis_index("dom")
    return lax.div(dom, 2 * ZS), lax.rem(lax.div(dom, 2), ZS), lax.rem(dom, 2)


def rank_of(offset, middle):
    return 2 * (offset - middle) if offset >= middle else 2 * (middle - offset) - 1


def chunk_x(dx, half):
    return 2 * (2 * rank_of(dx, XS // 2) + half) + 1


def chunk_z(dz):
    return 2 * rank_of(dz, ZS // 2)


def traced_rank(offset, middle):
    ahead = offset - middle
    return jnp.where(ahead >= 0, 2 * ahead, -2 * ahead - 1)


def build_kernel(
    count_ref, src_ref, dst_ref, tiles_ref, feats_ref, self_one_ref, neigh_one_ref, bias_one_ref, self_two_ref,
    neigh_two_ref, bias_two_ref, adj, feats_out, pack_out,
    tiles, src, dst, feats, self_one, neigh_one, bias_one, self_two, neigh_two, bias_two, total, order, cells, earlier,
    last, in_sems, small_sems,
):
    def load(source, target, n):
        copy = pltpu.make_async_copy(source, target, small_sems.at[n])
        copy.start()
        return copy

    index_loads = [load(src_ref, src, 0), load(dst_ref, dst, 1)]
    loads = []
    groups = TILES // GROUP
    for g in range(groups):
        part = pl.ds(g * GROUP, GROUP)
        loads.append(pltpu.make_async_copy(tiles_ref.at[part], tiles.at[part], in_sems.at[g]))
        loads[-1].start()
    weight_loads = [
        load(feats_ref, feats, 2), load(self_one_ref, self_one, 3), load(neigh_one_ref, neigh_one, 4),
        load(bias_one_ref, bias_one, 5), load(self_two_ref, self_two, 6), load(neigh_two_ref, neigh_two, 7),
        load(bias_two_ref, bias_two, 8),
    ]
    feat = lax.axis_index("feat")
    x, z, core = position()
    count = count_ref[0]

    def clear(i, carry):
        adj[i] = jnp.zeros(adj.shape[1:], BF16)
        return carry

    lax.fori_loop(0, adj.shape[0], clear, 0)

    def forget(i, carry):
        last[i] = -1
        return carry

    lax.fori_loop(0, 256, forget, 0, unroll=16)
    for copy in index_loads:
        copy.wait()

    def look(t, hits):
        to = dst[t]
        dom = lax.shift_right_logical(to, 2)
        other = lax.bitwise_xor(dom & 1, core)
        dz = (lax.shift_right_logical(dom, 1) - z) & (ZS - 1)
        dx = (lax.shift_right_logical(dom, 4) - x) & (XS - 1)
        mine = jnp.logical_and((to & 3) == feat, t < count)
        cell = jnp.where(mine, ((other * XS + dx) * ZS + dz) * 4 + src[t], 256)
        earlier[t] = last[cell]
        last[cell] = t
        order[hits] = t
        cells[hits] = cell
        return hits + mine.astype(jnp.int32)

    ends = [jnp.int32(0)]
    for g in range(groups):
        ends.append(lax.fori_loop(g * GROUP, (g + 1) * GROUP, look, ends[-1], unroll=8))

    for copy in weight_loads:
        copy.wait()
    feats_out[...] = feats[...].astype(F32)
    pack_out[0:32, :] = self_one[...].astype(F32)
    pack_out[32:64, :] = neigh_one[...].astype(F32)
    pack_out[64:72, :] = jnp.zeros((8, 256), F32)
    pack_out[64:65, 0:64] = bias_one[...]
    pack_out[65:66, 0:64] = bias_two[...]
    pack_out[72:136, :] = self_two[...].astype(F32)
    pack_out[136:200, :] = neigh_two[...].astype(F32)

    def put(cell, value):
        source = cell & 3
        dz = lax.shift_right_logical(cell, 2) & (ZS - 1)
        dx = lax.shift_right_logical(cell, 5) & (XS - 1)
        base = lax.shift_right_logical(cell, 7) * 16
        lanes = pl.ds(pl.multiple_of(source * BLK, BLK), BLK)
        rank_x, rank_z = traced_rank(dx, XS // 2), traced_rank(dz, ZS // 2)
        for half in range(2):
            chunk = base + 2 * (2 * rank_x + half) + 1
            rows = pl.ds(pl.multiple_of(rank_z * QUARTER, QUARTER), QUARTER)
            adj[chunk, rows, lanes] = value[half * QUARTER : (half + 1) * QUARTER]
        chunk = base + 2 * rank_z
        for half in range(2):
            rows = pl.ds(pl.multiple_of(half * BLK + rank_x * QUARTER, QUARTER), QUARTER)
            adj[chunk, rows, lanes] = value[64 + half * QUARTER : 64 + (half + 1) * QUARTER]

    def fill(i, carry):
        t = order[i]
        cell = cells[i]
        before = earlier[t]
        put(cell, tiles[t])

        @pl.when(jnp.logical_and(before >= 0, last[cell] == t))
        def _():
            total[...] = tiles[t].astype(F32)

            def more(at):
                total[...] += tiles[at].astype(F32)
                return earlier[at]

            lax.while_loop(lambda at: at >= 0, more, before)
            put(cell, total[...].astype(BF16))

        return carry

    for g in range(groups):
        loads[g].wait()
        lax.fori_loop(ends[g], ends[g + 1], fill, 0)


def build(src, dst, count, tiles, feats, self_one, neigh_one, bias_one, self_two, neigh_two, bias_two):
    vmem = pl.BlockSpec(memory_space=pltpu.VMEM)
    hbm = pl.BlockSpec(memory_space=pltpu.HBM)
    arrays = [src, dst, tiles, feats, self_one, neigh_one, bias_one, self_two, neigh_two, bias_two]
    arrays = [pltpu.with_memory_space_constraint(array, pltpu.HBM) for array in arrays]
    smem = [pltpu.SMEM((TILES + 8,), jnp.int32)] * 3 + [pltpu.SMEM((264,), jnp.int32)]
    return pl.pallas_call(
        build_kernel,
        out_shape=(
            pltpu.VMEM((32, 256, 512), BF16),
            pltpu.VMEM((32, 512), F32),
            pltpu.VMEM((PACK_ROWS, 256), F32),
        ),
        in_specs=[pl.BlockSpec(memory_space=pltpu.SMEM)] + [hbm] * 10,
        out_specs=(vmem, vmem, vmem),
        scratch_shapes=[
            pltpu.VMEM((TILES, BLK, BLK), BF16),
            pltpu.SMEM((TILES,), jnp.int32),
            pltpu.SMEM((TILES,), jnp.int32),
        ]
        + [pltpu.VMEM(array.shape, array.dtype) for array in arrays[3:]]
        + [pltpu.VMEM((BLK, BLK), F32)]
        + smem
        + [pltpu.SemaphoreType.DMA((TILES // GROUP,)), pltpu.SemaphoreType.DMA((9,))],
        compiler_params=pltpu.CompilerParams(vmem_limit_bytes=12 << 20),
    )(count, *arrays)


def add_up(into, terms):
    rows = into.shape[0]
    step = rows if rows <= 160 else BLK

    def body(i, carry):
        part = pl.ds(pl.multiple_of(i * step, step), step)
        value = terms[0][part, :]
        for term in terms[1:]:
            value = value + term[part, :]
        into[part, :] = value
        return carry

    if rows == step:
        body(0, 0)
    else:
        lax.fori_loop(0, rows // step, body, 0)


class Ring:
    def __init__(self, n, own, extra, land, up_id, down_id, sends, recvs, started):
        self.n, self.middle = n, n // 2
        self.own, self.extra, self.land = own, extra, land
        self.ids = (up_id, down_id)
        self.sends, self.recvs, self.started = sends, recvs, started

    def copy(self, way, distance, half):
        offset = distance if way == 0 else self.n - distance
        slot = (way * self.middle + distance - 1) * 2 + half
        return pltpu.make_async_remote_copy(
            src_ref=self.own(offset, half),
            dst_ref=self.land(way, distance - 1, half),
            send_sem=self.sends.at[slot],
            recv_sem=self.recvs.at[slot],
            device_id=self.ids[way],
            device_id_type=MESH,
        )

    def gather_terms(self, way, distance, half):
        first = self.middle if way == half else self.middle - 1
        if distance == first:
            return []
        self.copy(way, distance + 1, half).wait_recv()
        return [self.land(way, distance, half)]

    def send(self, way, distance, half):
        offset = distance if way == 0 else self.n - distance
        mine = self.own(offset, half)
        terms = [mine] + self.extra(offset, half) + self.gather_terms(way, distance, half)
        if len(terms) > 1:
            add_up(mine, terms)
        copy = self.copy(way, distance, half)
        copy.start()
        self.started.append(copy)

    def early(self, distance):
        self.send(0, distance, 1)
        self.send(1, distance, 0)

    def late(self, distance):
        self.send(0, distance, 0)
        self.send(1, distance, 1)

    def finish(self, half, into=None):
        mine = self.own(0, half)
        terms = [mine] + self.extra(0, half)
        for way in range(2):
            terms += self.gather_terms(way, 0, half)
        add_up(mine if into is None else into, terms)


class Direct:
    def __init__(self, n, own, landing, target_ids, sends, recvs, started):
        self.n, self.own, self.landing, self.ids = n, own, landing, target_ids
        self.sends, self.recvs, self.started = sends, recvs, started

    def copy(self, offset, half):
        slot = (offset - 1) * 2 + half
        return pltpu.make_async_remote_copy(
            src_ref=self.own(offset, half),
            dst_ref=self.landing.at[offset - 1, half],
            send_sem=self.sends.at[slot],
            recv_sem=self.recvs.at[slot],
            device_id=self.ids[offset - 1],
            device_id_type=MESH,
        )

    def send(self, offset):
        for half in range(2):
            copy = self.copy(offset, half)
            copy.start()
            self.started.append(copy)

    def finish(self, half, into):
        terms = [self.own(0, half)]
        for offset in range(1, self.n):
            self.copy(offset, half).wait_recv()
            terms.append(self.landing.at[offset - 1, half])
        add_up(into, terms)


def split(value):
    high = value.astype(BF16)
    rest = value - high.astype(F32)
    middle = rest.astype(BF16)
    low = (rest - middle.astype(F32)).astype(BF16)
    return high, middle, low


def dot(a, b):
    return jnp.dot(a, b, preferred_element_type=F32)


Z_GROUPS = ((0, 96), (96, 32))
X_GROUPS = ((0, 160), (160, 96))
TOGETHER = 2


def reduce_scatter(adj, rhs, bufs, sems, ids, started, after_start, before_end, on_z_rows, on_x_rows):
    sums, sent, got, z_up, z_down, x_up, x_down, tz_up, tz_down, tx_in = bufs
    pair_sends, pair_recvs, sends, recvs = sems
    pair_id, zp_id, zm_id, *x_ids = ids
    xp_id, xm_id = x_ids[0], x_ids[2]
    width = rhs.shape[1]

    def pair_copy(chunk):
        return pltpu.make_async_remote_copy(
            src_ref=sent.at[chunk], dst_ref=got.at[chunk], send_sem=pair_sends.at[chunk],
            recv_sem=pair_recvs.at[chunk], device_id=pair_id, device_id_type=MESH,
        )

    def product(first, target, at):
        lhs = adj[pl.ds(first, TOGETHER)].reshape(TOGETHER * 256, 512)
        target[pl.ds(at, TOGETHER)] = dot(lhs, rhs[...]).reshape(TOGETHER, 256, width)

    def for_pair(i, carry):
        product(16 + i * TOGETHER, sent, i * TOGETHER)
        for k in range(TOGETHER):
            pair_copy(i * TOGETHER + k).start()
        return carry

    def for_own(i, carry):
        product(i * TOGETHER, sums, i * TOGETHER)
        return carry

    def run(kind, first, end):
        lax.fori_loop(first // TOGETHER, end // TOGETHER, kind, 0)

    have = set()

    def arrived(chunk):
        if chunk not in have:
            have.add(chunk)
            pair_copy(chunk).wait_recv()

    def none(offset, half):
        return []

    def z_part(group):
        first, size = Z_GROUPS[group]

        def own(dz, half):
            return sums.at[chunk_z(dz), pl.ds(half * BLK + first, size)]

        def extra(dz, half):
            arrived(chunk_z(dz))
            return [got.at[chunk_z(dz), pl.ds(half * BLK + first, size)]]

        def land(way, at, half):
            return (z_up, z_down)[way].at[at, half, pl.ds(first, size)]

        slots = pl.ds(group * 16, 16)
        return Ring(ZS, own, extra, land, zp_id, zm_id, sends.at[slots], recvs.at[slots], started)

    def x_part(group):
        first, size = X_GROUPS[group]

        def own(dx, half):
            return sums.at[chunk_x(dx, half), pl.ds(first, size)]

        def extra(dx, half):
            arrived(chunk_x(dx, half))
            return [got.at[chunk_x(dx, half), pl.ds(first, size)]]

        def land(way, at, half):
            return (x_up, x_down)[way].at[at, half, pl.ds(first, size)]

        slots = pl.ds(32 + group * 8, 8)
        return Ring(XS, own, extra, land, xp_id, xm_id, sends.at[slots], recvs.at[slots], started)

    def last_z():
        def own(dz, half):
            return sums.at[chunk_x(0, half), pl.ds(rank_of(dz, ZS // 2) * QUARTER, QUARTER)]

        def land(way, at, half):
            return (tz_up, tz_down)[way].at[at, half]

        slots = pl.ds(48, 16)
        return Ring(ZS, own, none, land, zp_id, zm_id, sends.at[slots], recvs.at[slots], started)

    def last_x():
        def own(dx, half):
            return sums.at[chunk_z(0), pl.ds(half * BLK + rank_of(dx, XS // 2) * QUARTER, QUARTER)]

        return Direct(XS, own, tx_in, x_ids, sends.at[pl.ds(64, 6)], recvs.at[pl.ds(64, 6)], started)

    z0, z1, x0, x1, tz, tx = z_part(0), z_part(1), x_part(0), x_part(1), last_z(), last_x()

    run(for_pair, 0, 8)
    run(for_own, 0, 4)
    z0.late(4)
    x0.late(2)
    run(for_pair, 8, 12)
    run(for_own, 4, 8)
    z0.early(3)
    z1.late(4)
    z1.early(3)
    run(for_own, 8, 12)
    x0.early(1)
    run(for_pair, 12, 16)
    run(for_own, 12, 16)
    z0.late(3)
    x0.late(1)
    x1.late(2)
    x1.early(1)
    after_start()
    z0.early(2)
    z1.late(3)
    z0.late(2)
    z1.early(2)
    z0.early(1)
    x0.finish(0)
    x0.finish(1)
    tz.late(4)
    tz.early(3)
    z0.late(1)
    x1.late(1)
    z1.late(2)
    tz.late(3)
    z1.early(1)
    tz.early(2)
    z0.finish(0)
    z0.finish(1)
    for dx in (2, 1, 3):
        tx.send(dx)
    z1.late(1)
    tz.late(2)
    before_end()
    x1.finish(0)
    x1.finish(1)
    tz.early(1)
    tz.late(1)
    z1.finish(0)
    z1.finish(1)
    on_z_rows(tx)
    on_x_rows(tz)

    def drain(chunk, carry):
        pair_copy(chunk).wait_send()
        return carry

    return lambda: lax.fori_loop(0, 16, drain, 0)


def net_kernel(adj, feats_ref, pack_ref, out_ref, *scratch):
    (
        feats_all, packs, feats, hidden, self_one, neigh_one, self_two, neigh_two, bias, own_part, agg_all, agg_two, slices,
        landed, *rest
    ) = scratch
    bufs_one, bufs_two, rest = rest[:10], rest[10:20], rest[20:]
    y_sends, y_recvs, sems_one, sems_two = rest[0], rest[1], rest[2:6], rest[6:10]

    feat = lax.axis_index("feat")
    x, z, core = position()

    def at(x_at, z_at, core_at, feat_at=feat):
        return feat_at, (x_at * ZS + z_at) * 2 + core_at

    pair_id = at(x, z, 1 - core)
    zp_id, zm_id = at(x, lax.rem(z + 1, ZS), core), at(x, lax.rem(z + ZS - 1, ZS), core)
    x_ids = [at(lax.rem(x + k, XS), z, core) for k in range(1, XS)]
    y_ids = [at(x, z, core, lax.rem(feat + k, FS)) for k in range(1, FS)]
    ids = (pair_id, zp_id, zm_id, *x_ids)

    barrier = pltpu.get_barrier_semaphore()
    for other in ids + tuple(y_ids):
        pl.semaphore_signal(barrier, inc=1, device_id=other, device_id_type=MESH)
    pl.semaphore_wait(barrier, 9)

    started = []

    def to_y(kind, source, target):
        copies = []
        for k in range(1, FS):
            slot = kind * 3 + k - 1
            copies.append(
                pltpu.make_async_remote_copy(
                    src_ref=source(k), dst_ref=target, send_sem=y_sends.at[slot], recv_sem=y_recvs.at[slot],
                    device_id=y_ids[k - 1], device_id_type=MESH,
                )
            )
            copies[-1].start()
        if kind != 4:
            started.extend(copies)
        return copies

    def received(copies):
        for copy in copies:
            copy.wait_recv()

    feats_rows = pl.ds(pl.multiple_of(feat * 32, 32), 32)
    feats_copies = to_y(0, lambda k: feats_ref, feats_all.at[feats_rows])
    feats_all[feats_rows, :] = feats_ref[...]
    packs[feat] = pack_ref[...]
    received(feats_copies)
    feats[...] = feats_all[...].T.astype(BF16)

    pack_copies = []

    def send_pack(kind, first, size):
        rows = pl.ds(first, size)
        pack_copies.append(to_y(kind, lambda k: pack_ref.at[rows], packs.at[feat, rows]))

    def take_weights():
        received(pack_copies[0])
        low = lax.broadcasted_iota(jnp.int32, (1, BLK), 1) < 64
        for row in range(2):
            for pair in range(2):
                left = packs[2 * pair, 64 + row : 65 + row, 0:BLK]
                right = packs[2 * pair + 1, 64 + row : 65 + row, 0:BLK]
                value = jnp.where(low, left, pltpu.roll(right, 64, 1))
                bias[row : row + 1, pair * BLK : (pair + 1) * BLK] = value
        for j in range(FS):
            self_one[32 * j : 32 * (j + 1), :] = packs[j, 0:32, :].astype(BF16)
            neigh_one[32 * j : 32 * (j + 1), :] = packs[j, 32:64, :].astype(BF16)

        own_part[...] = dot(feats[...], self_one[...]) + bias[0:1, :]

    own = pl.ds(pl.multiple_of(feat * BLK, BLK), BLK)

    def own_of_two():
        received(pack_copies[1])
        for j in range(FS):
            self_two[64 * j : 64 * (j + 1), :] = packs[j, 72:136, :].astype(BF16)
            neigh_two[64 * j : 64 * (j + 1), :] = packs[j, 136:200, :].astype(BF16)
        own_part[0:BLK, :] = dot(hidden[own, :], self_two[...]) + bias[1:2, :]

    agg_copies = []

    def share(kind, rows, ring):
        for half in range(2):
            ring.finish(half, agg_all.at[feat, pl.ds(rows + half * QUARTER, QUARTER)])
        part = agg_all.at[feat, pl.ds(rows, 64)]
        agg_copies.extend(to_y(kind, lambda k: part, part))

    drain_one = reduce_scatter(
        adj, feats, bufs_one, sems_one, ids, started, lambda: send_pack(1, 0, 72), take_weights,
        lambda ring: share(2, 64, ring), lambda ring: share(3, 0, ring),
    )
    received(agg_copies)

    def hide(j, carry):
        rows = pl.ds(pl.multiple_of(j * BLK, BLK), BLK)
        pre = own_part[rows, :]
        for part in split(agg_all[j]):
            pre = pre + dot(part, neigh_one[...])
        hidden[rows, :] = jnp.maximum(pre, 0.0).astype(BF16)
        return carry

    lax.fori_loop(0, FS, hide, 0)

    def keep(rows, ring):
        for half in range(2):
            ring.finish(half, agg_two.at[pl.ds(rows + half * QUARTER, QUARTER)])

    drain_two = reduce_scatter(
        adj, hidden, bufs_two, sems_two, ids, started, lambda: send_pack(5, 72, 128), own_of_two,
        lambda ring: keep(64, ring), lambda ring: keep(0, ring),
    )

    pre = own_part[0:BLK, :]
    for part in split(agg_two[...]):
        pre = pre + dot(part, neigh_two[...])
    result = jnp.maximum(pre, 0.0)
    slices[...] = result.T.reshape(FS, 64, BLK)
    out_copies = to_y(4, lambda k: slices.at[lax.rem(feat + k, FS)], landed.at[feat])
    landed[feat] = slices[feat]
    drain_one()
    drain_two()
    for copy in started:
        copy.wait_send()
    received(out_copies)
    for j in range(FS):
        out_ref[:, j * BLK : (j + 1) * BLK] = landed[j].astype(BF16)

    for copy in out_copies:
        copy.wait_send()


def layer_buffers(width):
    shapes = [(16, 256, width)] * 3
    shapes += [(4, 2, 128, width)] * 2 + [(2, 2, 256, width)] * 2 + [(4, 2, 32, width)] * 2 + [(3, 2, 32, width)]
    return [pltpu.VMEM(shape, F32) for shape in shapes]


def net(adj, feats, pack):
    vmem = pl.BlockSpec(memory_space=pltpu.VMEM)
    dma = pltpu.SemaphoreType.DMA
    return pl.pallas_call(
        net_kernel,
        out_shape=jax.ShapeDtypeStruct((64, 512), BF16),
        in_specs=[vmem] * 3,
        out_specs=vmem,
        scratch_shapes=[
            pltpu.VMEM((128, 512), F32),
            pltpu.VMEM((FS, PACK_ROWS, 256), F32),
            pltpu.VMEM((512, 128), BF16),
            pltpu.VMEM((512, 256), BF16),
            pltpu.VMEM((128, 256), BF16),
            pltpu.VMEM((128, 256), BF16),
            pltpu.VMEM((256, 256), BF16),
            pltpu.VMEM((256, 256), BF16),
            pltpu.VMEM((8, 256), F32),
            pltpu.VMEM((512, 256), F32),
            pltpu.VMEM((FS, 128, 128), F32),
            pltpu.VMEM((128, 256), F32),
            pltpu.VMEM((FS, 64, 128), F32),
            pltpu.VMEM((FS, 64, 128), F32),
        ]
        + layer_buffers(128)
        + layer_buffers(256)
        + [dma((18,)), dma((18,))]
        + [dma((16,)), dma((16,)), dma((72,)), dma((72,))] * 2,
        compiler_params=pltpu.CompilerParams(
            collective_id=0, has_side_effects=True, vmem_limit_bytes=36 << 20
        ),
    )(*[pltpu.with_memory_space_constraint(array, pltpu.VMEM) for array in (adj, feats, pack)])


def on_device(
    feats, tile_src, tile_dst, tile_val, tile_count, self_one, neigh_one, bias_one, self_two, neigh_two, bias_two
):
    adj, columns, pack = build(
        tile_src, tile_dst, tile_count, tile_val, feats.T, self_one, neigh_one, bias_one.reshape(1, 64), self_two,
        neigh_two, bias_two.reshape(1, 64),
    )
    return net(adj, columns, pack).T


def solution(mesh):
    placed = (
        P("dom", "feat"),
        P("dom"),
        P("dom"),
        P("dom", None, None),
        P("dom"),
        P("feat", None),
        P("feat", None),
        P("feat"),
        P("feat", None),
        P("feat", None),
        P("feat"),
    )
    return jax.shard_map(
        on_device, mesh=mesh, in_specs=placed, out_specs=P("dom", "feat"), check_vma=False
    )
```

```python
import functools

import jax
import jax.numpy as jnp
from jax import lax
from jax.experimental import pallas as pl
from jax.experimental.pallas import tpu as pltpu
from jax.sharding import PartitionSpec as P

MESH = pl.DeviceIdType.MESH
BLK = 128
QUARTER = 32
XS, ZS, FS = 4, 8, 4
TILES = 256
GROUP = 32
PACK_ROWS = 200
F32, BF16 = jnp.float32, jnp.bfloat16


def position():
    dom = lax.axis_index("dom")
    return lax.div(dom, 2 * ZS), lax.rem(lax.div(dom, 2), ZS), lax.rem(dom, 2)


def rank_of(offset, middle):
    return 2 * (offset - middle) if offset >= middle else 2 * (middle - offset) - 1


def chunk_x(dx, half):
    return 2 * (2 * rank_of(dx, XS // 2) + half) + 1


def chunk_z(dz):
    return 2 * rank_of(dz, ZS // 2)


def traced_rank(offset, middle):
    ahead = offset - middle
    return jnp.where(ahead >= 0, 2 * ahead, -2 * ahead - 1)


def build_kernel(
    count_ref, src_ref, dst_ref, tiles_ref, feats_ref, self_one_ref, neigh_one_ref, bias_one_ref, self_two_ref,
    neigh_two_ref, bias_two_ref, adj, feats_out, pack_out,
    tiles, src, dst, feats, self_one, neigh_one, bias_one, self_two, neigh_two, bias_two, total, order, cells, earlier,
    last, in_sems, small_sems,
):
    def load(source, target, n):
        copy = pltpu.make_async_copy(source, target, small_sems.at[n])
        copy.start()
        return copy

    index_loads = [load(src_ref, src, 0), load(dst_ref, dst, 1)]
    loads = []
    groups = TILES // GROUP
    for g in range(groups):
        part = pl.ds(g * GROUP, GROUP)
        loads.append(pltpu.make_async_copy(tiles_ref.at[part], tiles.at[part], in_sems.at[g]))
        loads[-1].start()
    weight_loads = [
        load(feats_ref, feats, 2), load(self_one_ref, self_one, 3), load(neigh_one_ref, neigh_one, 4),
        load(bias_one_ref, bias_one, 5), load(self_two_ref, self_two, 6), load(neigh_two_ref, neigh_two, 7),
        load(bias_two_ref, bias_two, 8),
    ]
    feat = lax.axis_index("feat")
    x, z, core = position()
    count = count_ref[0]

    def clear(i, carry):
        adj[i] = jnp.zeros(adj.shape[1:], BF16)
        return carry

    lax.fori_loop(0, adj.shape[0], clear, 0)

    def forget(i, carry):
        last[i] = -1
        return carry

    lax.fori_loop(0, 256, forget, 0, unroll=16)
    for copy in index_loads:
        copy.wait()

    def look(t, hits):
        to = dst[t]
        dom = lax.shift_right_logical(to, 2)
        other = lax.bitwise_xor(dom & 1, core)
        dz = (lax.shift_right_logical(dom, 1) - z) & (ZS - 1)
        dx = (lax.shift_right_logical(dom, 4) - x) & (XS - 1)
        mine = jnp.logical_and((to & 3) == feat, t < count)
        cell = jnp.where(mine, ((other * XS + dx) * ZS + dz) * 4 + src[t], 256)
        earlier[t] = last[cell]
        last[cell] = t
        order[hits] = t
        cells[hits] = cell
        return hits + mine.astype(jnp.int32)

    ends = [jnp.int32(0)]
    for g in range(groups):
        ends.append(lax.fori_loop(g * GROUP, (g + 1) * GROUP, look, ends[-1], unroll=8))

    for copy in weight_loads:
        copy.wait()
    feats_out[...] = feats[...].astype(F32)
    pack_out[0:32, :] = self_one[...].astype(F32)
    pack_out[32:64, :] = neigh_one[...].astype(F32)
    pack_out[64:72, :] = jnp.zeros((8, 256), F32)
    pack_out[64:65, 0:64] = bias_one[...]
    pack_out[65:66, 0:64] = bias_two[...]
    pack_out[72:136, :] = self_two[...].astype(F32)
    pack_out[136:200, :] = neigh_two[...].astype(F32)

    def put(cell, value):
        source = cell & 3
        dz = lax.shift_right_logical(cell, 2) & (ZS - 1)
        dx = lax.shift_right_logical(cell, 5) & (XS - 1)
        base = lax.shift_right_logical(cell, 7) * 16
        lanes = pl.ds(pl.multiple_of(source * BLK, BLK), BLK)
        rank_x, rank_z = traced_rank(dx, XS // 2), traced_rank(dz, ZS // 2)
        for half in range(2):
            chunk = base + 2 * (2 * rank_x + half) + 1
            rows = pl.ds(pl.multiple_of(rank_z * QUARTER, QUARTER), QUARTER)
            adj[chunk, rows, lanes] = value[half * QUARTER : (half + 1) * QUARTER]
        chunk = base + 2 * rank_z
        for half in range(2):
            rows = pl.ds(pl.multiple_of(half * BLK + rank_x * QUARTER, QUARTER), QUARTER)
            adj[chunk, rows, lanes] = value[64 + half * QUARTER : 64 + (half + 1) * QUARTER]

    def fill(i, carry):
        t = order[i]
        cell = cells[i]
        before = earlier[t]
        put(cell, tiles[t])

        @pl.when(jnp.logical_and(before >= 0, last[cell] == t))
        def _():
            total[...] = tiles[t].astype(F32)

            def more(at):
                total[...] += tiles[at].astype(F32)
                return earlier[at]

            lax.while_loop(lambda at: at >= 0, more, before)
            put(cell, total[...].astype(BF16))

        return carry

    for g in range(groups):
        loads[g].wait()
        lax.fori_loop(ends[g], ends[g + 1], fill, 0)


def build(src, dst, count, tiles, feats, self_one, neigh_one, bias_one, self_two, neigh_two, bias_two):
    vmem = pl.BlockSpec(memory_space=pltpu.VMEM)
    hbm = pl.BlockSpec(memory_space=pltpu.HBM)
    arrays = [src, dst, tiles, feats, self_one, neigh_one, bias_one, self_two, neigh_two, bias_two]
    arrays = [pltpu.with_memory_space_constraint(array, pltpu.HBM) for array in arrays]
    smem = [pltpu.SMEM((TILES + 8,), jnp.int32)] * 3 + [pltpu.SMEM((264,), jnp.int32)]
    return pl.pallas_call(
        build_kernel,
        out_shape=(
            pltpu.VMEM((32, 256, 512), BF16),
            pltpu.VMEM((32, 512), F32),
            pltpu.VMEM((PACK_ROWS, 256), F32),
        ),
        in_specs=[pl.BlockSpec(memory_space=pltpu.SMEM)] + [hbm] * 10,
        out_specs=(vmem, vmem, vmem),
        scratch_shapes=[
            pltpu.VMEM((TILES, BLK, BLK), BF16),
            pltpu.SMEM((TILES,), jnp.int32),
            pltpu.SMEM((TILES,), jnp.int32),
        ]
        + [pltpu.VMEM(array.shape, array.dtype) for array in arrays[3:]]
        + [pltpu.VMEM((BLK, BLK), F32)]
        + smem
        + [pltpu.SemaphoreType.DMA((TILES // GROUP,)), pltpu.SemaphoreType.DMA((9,))],
        compiler_params=pltpu.CompilerParams(vmem_limit_bytes=12 << 20),
    )(count, *arrays)


def add_up(into, terms):
    rows = into.shape[0]
    step = rows if rows <= 160 else BLK

    def body(i, carry):
        part = pl.ds(pl.multiple_of(i * step, step), step)
        value = terms[0][part, :]
        for term in terms[1:]:
            value = value + term[part, :]
        into[part, :] = value
        return carry

    if rows == step:
        body(0, 0)
    else:
        lax.fori_loop(0, rows // step, body, 0)


class Ring:
    def __init__(self, n, own, extra, land, up_id, down_id, sends, recvs, started):
        self.n, self.middle = n, n // 2
        self.own, self.extra, self.land = own, extra, land
        self.ids = (up_id, down_id)
        self.sends, self.recvs, self.started = sends, recvs, started

    def copy(self, way, distance, half):
        offset = distance if way == 0 else self.n - distance
        slot = (way * self.middle + distance - 1) * 2 + half
        return pltpu.make_async_remote_copy(
            src_ref=self.own(offset, half),
            dst_ref=self.land(way, distance - 1, half),
            send_sem=self.sends.at[slot],
            recv_sem=self.recvs.at[slot],
            device_id=self.ids[way],
            device_id_type=MESH,
        )

    def gather_terms(self, way, distance, half):
        first = self.middle if way == half else self.middle - 1
        if distance == first:
            return []
        self.copy(way, distance + 1, half).wait_recv()
        return [self.land(way, distance, half)]

    def send(self, way, distance, half):
        offset = distance if way == 0 else self.n - distance
        mine = self.own(offset, half)
        terms = [mine] + self.extra(offset, half) + self.gather_terms(way, distance, half)
        if len(terms) > 1:
            add_up(mine, terms)
        copy = self.copy(way, distance, half)
        copy.start()
        self.started.append(copy)

    def early(self, distance):
        self.send(0, distance, 1)
        self.send(1, distance, 0)

    def late(self, distance):
        self.send(0, distance, 0)
        self.send(1, distance, 1)

    def finish(self, half, into=None):
        mine = self.own(0, half)
        terms = [mine] + self.extra(0, half)
        for way in range(2):
            terms += self.gather_terms(way, 0, half)
        add_up(mine if into is None else into, terms)


class Direct:
    def __init__(self, n, own, landing, target_ids, sends, recvs, started):
        self.n, self.own, self.landing, self.ids = n, own, landing, target_ids
        self.sends, self.recvs, self.started = sends, recvs, started

    def copy(self, offset, half):
        slot = (offset - 1) * 2 + half
        return pltpu.make_async_remote_copy(
            src_ref=self.own(offset, half),
            dst_ref=self.landing.at[offset - 1, half],
            send_sem=self.sends.at[slot],
            recv_sem=self.recvs.at[slot],
            device_id=self.ids[offset - 1],
            device_id_type=MESH,
        )

    def send(self, offset):
        for half in range(2):
            copy = self.copy(offset, half)
            copy.start()
            self.started.append(copy)

    def finish(self, half, into):
        terms = [self.own(0, half)]
        for offset in range(1, self.n):
            self.copy(offset, half).wait_recv()
            terms.append(self.landing.at[offset - 1, half])
        add_up(into, terms)


def split(value):
    high = value.astype(BF16)
    rest = value - high.astype(F32)
    middle = rest.astype(BF16)
    low = (rest - middle.astype(F32)).astype(BF16)
    return high, middle, low


def dot(a, b):
    return jnp.dot(a, b, preferred_element_type=F32)


Z_GROUPS = ((0, 96), (96, 32))
X_GROUPS = ((0, 96), (96, 64), (160, 96))
TOGETHER = 2


def reduce_scatter(adj, rhs, bufs, sems, ids, started, after_start, before_end, on_z_rows, on_x_rows):
    sums, sent, got, z_up, z_down, x_up, x_down, tz_up, tz_down, tx_in = bufs
    pair_sends, pair_recvs, sends, recvs = sems
    pair_id, zp_id, zm_id, *x_ids = ids
    xp_id, xm_id = x_ids[0], x_ids[2]
    width = rhs.shape[1]

    def pair_copy(chunk):
        return pltpu.make_async_remote_copy(
            src_ref=sent.at[chunk], dst_ref=got.at[chunk], send_sem=pair_sends.at[chunk],
            recv_sem=pair_recvs.at[chunk], device_id=pair_id, device_id_type=MESH,
        )

    def product(first, target, at):
        lhs = adj[pl.ds(first, TOGETHER)].reshape(TOGETHER * 256, 512)
        target[pl.ds(at, TOGETHER)] = dot(lhs, rhs[...]).reshape(TOGETHER, 256, width)

    def for_pair(i, carry):
        product(16 + i * TOGETHER, sent, i * TOGETHER)
        for k in range(TOGETHER):
            pair_copy(i * TOGETHER + k).start()
        return carry

    def for_own(i, carry):
        product(i * TOGETHER, sums, i * TOGETHER)
        return carry

    def run(kind, first, end):
        lax.fori_loop(first // TOGETHER, end // TOGETHER, kind, 0)

    have = set()

    def arrived(chunk):
        if chunk not in have:
            have.add(chunk)
            pair_copy(chunk).wait_recv()

    def none(offset, half):
        return []

    def z_part(group):
        first, size = Z_GROUPS[group]

        def own(dz, half):
            return sums.at[chunk_z(dz), pl.ds(half * BLK + first, size)]

        def extra(dz, half):
            arrived(chunk_z(dz))
            return [got.at[chunk_z(dz), pl.ds(half * BLK + first, size)]]

        def land(way, at, half):
            return (z_up, z_down)[way].at[at, half, pl.ds(first, size)]

        slots = pl.ds(group * 16, 16)
        return Ring(ZS, own, extra, land, zp_id, zm_id, sends.at[slots], recvs.at[slots], started)

    def x_part(group):
        first, size = X_GROUPS[group]

        def own(dx, half):
            return sums.at[chunk_x(dx, half), pl.ds(first, size)]

        def extra(dx, half):
            arrived(chunk_x(dx, half))
            return [got.at[chunk_x(dx, half), pl.ds(first, size)]]

        def land(way, at, half):
            return (x_up, x_down)[way].at[at, half, pl.ds(first, size)]

        slots = pl.ds(32 + group * 8, 8)
        return Ring(XS, own, extra, land, xp_id, xm_id, sends.at[slots], recvs.at[slots], started)

    def last_z():
        def own(dz, half):
            return sums.at[chunk_x(0, half), pl.ds(rank_of(dz, ZS // 2) * QUARTER, QUARTER)]

        def land(way, at, half):
            return (tz_up, tz_down)[way].at[at, half]

        slots = pl.ds(56, 16)
        return Ring(ZS, own, none, land, zp_id, zm_id, sends.at[slots], recvs.at[slots], started)

    def last_x():
        def own(dx, half):
            return sums.at[chunk_z(0), pl.ds(half * BLK + rank_of(dx, XS // 2) * QUARTER, QUARTER)]

        return Direct(XS, own, tx_in, x_ids, sends.at[pl.ds(72, 6)], recvs.at[pl.ds(72, 6)], started)

    z0, z1, x0, x1, x2, tz, tx = z_part(0), z_part(1), x_part(0), x_part(1), x_part(2), last_z(), last_x()

    run(for_pair, 0, 8)
    run(for_own, 0, 4)
    z0.late(4)
    x0.late(2)
    run(for_pair, 8, 12)
    run(for_own, 4, 8)
    z0.early(3)
    z1.late(4)
    z1.early(3)
    run(for_own, 8, 12)
    x0.early(1)
    run(for_pair, 12, 16)
    run(for_own, 12, 16)
    z0.late(3)
    x0.late(1)
    x1.late(2)
    x1.early(1)
    after_start()
    z0.early(2)
    z1.late(3)
    x0.finish(0)
    x0.finish(1)
    tz.late(4)
    tz.early(3)
    z0.late(2)
    x1.late(1)
    x2.late(2)
    x2.early(1)
    z1.early(2)
    z0.early(1)
    tz.late(3)
    x1.finish(0)
    x1.finish(1)
    tz.early(2)
    z0.late(1)
    z1.late(2)
    x2.late(1)
    tz.late(2)
    z1.early(1)
    z0.finish(0)
    z0.finish(1)
    for dx in (2, 1, 3):
        tx.send(dx)
    z1.late(1)
    before_end()
    x2.finish(0)
    x2.finish(1)
    tz.early(1)
    tz.late(1)
    z1.finish(0)
    z1.finish(1)
    on_z_rows(tx)
    on_x_rows(tz)

    def drain(chunk, carry):
        pair_copy(chunk).wait_send()
        return carry

    return lambda: lax.fori_loop(0, 16, drain, 0)


def net_kernel(adj, feats_ref, pack_ref, out_ref, *scratch):
    (
        feats_all, packs, feats, hidden, self_one, neigh_one, self_two, neigh_two, bias, own_part, agg_all, agg_two, slices,
        landed, *rest
    ) = scratch
    bufs_one, bufs_two, rest = rest[:10], rest[10:20], rest[20:]
    y_sends, y_recvs, sems_one, sems_two = rest[0], rest[1], rest[2:6], rest[6:10]

    feat = lax.axis_index("feat")
    x, z, core = position()

    def at(x_at, z_at, core_at, feat_at=feat):
        return feat_at, (x_at * ZS + z_at) * 2 + core_at

    pair_id = at(x, z, 1 - core)
    zp_id, zm_id = at(x, lax.rem(z + 1, ZS), core), at(x, lax.rem(z + ZS - 1, ZS), core)
    x_ids = [at(lax.rem(x + k, XS), z, core) for k in range(1, XS)]
    y_ids = [at(x, z, core, lax.rem(feat + k, FS)) for k in range(1, FS)]
    ids = (pair_id, zp_id, zm_id, *x_ids)

    barrier = pltpu.get_barrier_semaphore()
    for other in ids + tuple(y_ids):
        pl.semaphore_signal(barrier, inc=1, device_id=other, device_id_type=MESH)
    pl.semaphore_wait(barrier, 9)

    started = []

    def to_y(kind, source, target):
        copies = []
        for k in range(1, FS):
            slot = kind * 3 + k - 1
            copies.append(
                pltpu.make_async_remote_copy(
                    src_ref=source(k), dst_ref=target, send_sem=y_sends.at[slot], recv_sem=y_recvs.at[slot],
                    device_id=y_ids[k - 1], device_id_type=MESH,
                )
            )
            copies[-1].start()
        if kind != 4:
            started.extend(copies)
        return copies

    def received(copies):
        for copy in copies:
            copy.wait_recv()

    feats_rows = pl.ds(pl.multiple_of(feat * 32, 32), 32)
    feats_copies = to_y(0, lambda k: feats_ref, feats_all.at[feats_rows])
    feats_all[feats_rows, :] = feats_ref[...]
    packs[feat] = pack_ref[...]
    received(feats_copies)
    feats[...] = feats_all[...].T.astype(BF16)

    pack_copies = []

    def send_pack(kind, first, size):
        rows = pl.ds(first, size)
        pack_copies.append(to_y(kind, lambda k: pack_ref.at[rows], packs.at[feat, rows]))

    def take_weights():
        received(pack_copies[0])
        low = lax.broadcasted_iota(jnp.int32, (1, BLK), 1) < 64
        for row in range(2):
            for pair in range(2):
                left = packs[2 * pair, 64 + row : 65 + row, 0:BLK]
                right = packs[2 * pair + 1, 64 + row : 65 + row, 0:BLK]
                value = jnp.where(low, left, pltpu.roll(right, 64, 1))
                bias[row : row + 1, pair * BLK : (pair + 1) * BLK] = value
        for j in range(FS):
            self_one[32 * j : 32 * (j + 1), :] = packs[j, 0:32, :].astype(BF16)
            neigh_one[32 * j : 32 * (j + 1), :] = packs[j, 32:64, :].astype(BF16)

        own_part[...] = dot(feats[...], self_one[...]) + bias[0:1, :]

    own = pl.ds(pl.multiple_of(feat * BLK, BLK), BLK)

    def own_of_two():
        received(pack_copies[1])
        for j in range(FS):
            self_two[64 * j : 64 * (j + 1), :] = packs[j, 72:136, :].astype(BF16)
            neigh_two[64 * j : 64 * (j + 1), :] = packs[j, 136:200, :].astype(BF16)
        own_part[0:BLK, :] = dot(hidden[own, :], self_two[...]) + bias[1:2, :]

    agg_copies = []

    def share(kind, rows, ring):
        for half in range(2):
            ring.finish(half, agg_all.at[feat, pl.ds(rows + half * QUARTER, QUARTER)])
        part = agg_all.at[feat, pl.ds(rows, 64)]
        agg_copies.extend(to_y(kind, lambda k: part, part))

    drain_one = reduce_scatter(
        adj, feats, bufs_one, sems_one, ids, started, lambda: send_pack(1, 0, 72), take_weights,
        lambda ring: share(2, 64, ring), lambda ring: share(3, 0, ring),
    )
    received(agg_copies)

    pre = own_part[...]
    for part in split(agg_all[...].reshape(FS * BLK, BLK)):
        pre = pre + dot(part, neigh_one[...])
    hidden[...] = jnp.maximum(pre, 0.0).astype(BF16)

    def keep(rows, ring):
        for half in range(2):
            ring.finish(half, agg_two.at[pl.ds(rows + half * QUARTER, QUARTER)])

    drain_two = reduce_scatter(
        adj, hidden, bufs_two, sems_two, ids, started, lambda: send_pack(5, 72, 128), own_of_two,
        lambda ring: keep(64, ring), lambda ring: keep(0, ring),
    )

    pre = own_part[0:BLK, :]
    for part in split(agg_two[...]):
        pre = pre + dot(part, neigh_two[...])
    result = jnp.maximum(pre, 0.0)
    slices[...] = result.T.reshape(FS, 64, BLK)
    out_copies = to_y(4, lambda k: slices.at[lax.rem(feat + k, FS)], landed.at[feat])
    landed[feat] = slices[feat]
    drain_one()
    drain_two()
    for copy in started:
        copy.wait_send()
    received(out_copies)
    for j in range(FS):
        out_ref[:, j * BLK : (j + 1) * BLK] = landed[j].astype(BF16)

    for copy in out_copies:
        copy.wait_send()


def layer_buffers(width):
    shapes = [(16, 256, width)] * 3
    shapes += [(4, 2, 128, width)] * 2 + [(2, 2, 256, width)] * 2 + [(4, 2, 32, width)] * 2 + [(3, 2, 32, width)]
    return [pltpu.VMEM(shape, F32) for shape in shapes]


def net(adj, feats, pack):
    vmem = pl.BlockSpec(memory_space=pltpu.VMEM)
    dma = pltpu.SemaphoreType.DMA
    return pl.pallas_call(
        net_kernel,
        out_shape=jax.ShapeDtypeStruct((64, 512), BF16),
        in_specs=[vmem] * 3,
        out_specs=vmem,
        scratch_shapes=[
            pltpu.VMEM((128, 512), F32),
            pltpu.VMEM((FS, PACK_ROWS, 256), F32),
            pltpu.VMEM((512, 128), BF16),
            pltpu.VMEM((512, 256), BF16),
            pltpu.VMEM((128, 256), BF16),
            pltpu.VMEM((128, 256), BF16),
            pltpu.VMEM((256, 256), BF16),
            pltpu.VMEM((256, 256), BF16),
            pltpu.VMEM((8, 256), F32),
            pltpu.VMEM((512, 256), F32),
            pltpu.VMEM((FS, 128, 128), F32),
            pltpu.VMEM((128, 256), F32),
            pltpu.VMEM((FS, 64, 128), F32),
            pltpu.VMEM((FS, 64, 128), F32),
        ]
        + layer_buffers(128)
        + layer_buffers(256)
        + [dma((18,)), dma((18,))]
        + [dma((16,)), dma((16,)), dma((80,)), dma((80,))] * 2,
        compiler_params=pltpu.CompilerParams(
            collective_id=0, has_side_effects=True, vmem_limit_bytes=36 << 20
        ),
    )(*[pltpu.with_memory_space_constraint(array, pltpu.VMEM) for array in (adj, feats, pack)])


def on_device(
    feats, tile_src, tile_dst, tile_val, tile_count, self_one, neigh_one, bias_one, self_two, neigh_two, bias_two
):
    adj, columns, pack = build(
        tile_src, tile_dst, tile_count, tile_val, feats.T, self_one, neigh_one, bias_one.reshape(1, 64), self_two,
        neigh_two, bias_two.reshape(1, 64),
    )
    return net(adj, columns, pack).T


def solution(mesh):
    placed = (
        P("dom", "feat"),
        P("dom"),
        P("dom"),
        P("dom", None, None),
        P("dom"),
        P("feat", None),
        P("feat", None),
        P("feat"),
        P("feat", None),
        P("feat", None),
        P("feat"),
    )
    return jax.shard_map(
        on_device, mesh=mesh, in_specs=placed, out_specs=P("dom", "feat"), check_vma=False
    )
```

```python
import functools

import jax
import jax.numpy as jnp
from jax import lax
from jax.experimental import pallas as pl
from jax.experimental.pallas import tpu as pltpu
from jax.sharding import PartitionSpec as P

MESH = pl.DeviceIdType.MESH
BLK = 128
QUARTER = 32
XS, ZS, FS = 4, 8, 4
TILES = 256
GROUP = 32
PACK_ROWS = 200
F32, BF16 = jnp.float32, jnp.bfloat16


def position():
    dom = lax.axis_index("dom")
    return lax.div(dom, 2 * ZS), lax.rem(lax.div(dom, 2), ZS), lax.rem(dom, 2)


def rank_of(offset, middle):
    return 2 * (offset - middle) if offset >= middle else 2 * (middle - offset) - 1


def chunk_x(dx, half):
    return 2 * (2 * rank_of(dx, XS // 2) + half) + 1


def chunk_z(dz):
    return 2 * rank_of(dz, ZS // 2)


def traced_rank(offset, middle):
    ahead = offset - middle
    return jnp.where(ahead >= 0, 2 * ahead, -2 * ahead - 1)


def build_kernel(
    count_ref, src_ref, dst_ref, tiles_ref, feats_ref, self_one_ref, neigh_one_ref, bias_one_ref, self_two_ref,
    neigh_two_ref, bias_two_ref, adj, feats_out, pack_out,
    tiles, src, dst, feats, self_one, neigh_one, bias_one, self_two, neigh_two, bias_two, total, order, cells, earlier,
    last, in_sems, small_sems,
):
    def load(source, target, n):
        copy = pltpu.make_async_copy(source, target, small_sems.at[n])
        copy.start()
        return copy

    index_loads = [load(src_ref, src, 0), load(dst_ref, dst, 1)]
    loads = []
    groups = TILES // GROUP
    for g in range(groups):
        part = pl.ds(g * GROUP, GROUP)
        loads.append(pltpu.make_async_copy(tiles_ref.at[part], tiles.at[part], in_sems.at[g]))
        loads[-1].start()
    weight_loads = [
        load(feats_ref, feats, 2), load(self_one_ref, self_one, 3), load(neigh_one_ref, neigh_one, 4),
        load(bias_one_ref, bias_one, 5), load(self_two_ref, self_two, 6), load(neigh_two_ref, neigh_two, 7),
        load(bias_two_ref, bias_two, 8),
    ]
    feat = lax.axis_index("feat")
    x, z, core = position()
    count = count_ref[0]

    def clear(i, carry):
        adj[i] = jnp.zeros(adj.shape[1:], BF16)
        return carry

    lax.fori_loop(0, adj.shape[0], clear, 0)

    def forget(i, carry):
        last[i] = -1
        return carry

    lax.fori_loop(0, 256, forget, 0, unroll=16)
    for copy in index_loads:
        copy.wait()

    def look(t, hits):
        to = dst[t]
        dom = lax.shift_right_logical(to, 2)
        other = lax.bitwise_xor(dom & 1, core)
        dz = (lax.shift_right_logical(dom, 1) - z) & (ZS - 1)
        dx = (lax.shift_right_logical(dom, 4) - x) & (XS - 1)
        mine = jnp.logical_and((to & 3) == feat, t < count)
        cell = jnp.where(mine, ((other * XS + dx) * ZS + dz) * 4 + src[t], 256)
        earlier[t] = last[cell]
        last[cell] = t
        order[hits] = t
        cells[hits] = cell
        return hits + mine.astype(jnp.int32)

    ends = [jnp.int32(0)]
    for g in range(groups):
        ends.append(lax.fori_loop(g * GROUP, (g + 1) * GROUP, look, ends[-1], unroll=8))

    for copy in weight_loads:
        copy.wait()
    feats_out[...] = feats[...].astype(F32)
    pack_out[0:32, :] = self_one[...].astype(F32)
    pack_out[32:64, :] = neigh_one[...].astype(F32)
    pack_out[64:72, :] = jnp.zeros((8, 256), F32)
    pack_out[64:65, 0:64] = bias_one[...]
    pack_out[65:66, 0:64] = bias_two[...]
    pack_out[72:136, :] = self_two[...].astype(F32)
    pack_out[136:200, :] = neigh_two[...].astype(F32)

    def put(cell, value):
        source = cell & 3
        dz = lax.shift_right_logical(cell, 2) & (ZS - 1)
        dx = lax.shift_right_logical(cell, 5) & (XS - 1)
        base = lax.shift_right_logical(cell, 7) * 16
        lanes = pl.ds(pl.multiple_of(source * BLK, BLK), BLK)
        rank_x, rank_z = traced_rank(dx, XS // 2), traced_rank(dz, ZS // 2)
        for half in range(2):
            chunk = base + 2 * (2 * rank_x + half) + 1
            rows = pl.ds(pl.multiple_of(rank_z * QUARTER, QUARTER), QUARTER)
            adj[chunk, rows, lanes] = value[half * QUARTER : (half + 1) * QUARTER]
        chunk = base + 2 * rank_z
        for half in range(2):
            rows = pl.ds(pl.multiple_of(half * BLK + rank_x * QUARTER, QUARTER), QUARTER)
            adj[chunk, rows, lanes] = value[64 + half * QUARTER : 64 + (half + 1) * QUARTER]

    def fill(i, carry):
        t = order[i]
        cell = cells[i]
        before = earlier[t]
        put(cell, tiles[t])

        @pl.when(jnp.logical_and(before >= 0, last[cell] == t))
        def _():
            total[...] = tiles[t].astype(F32)

            def more(at):
                total[...] += tiles[at].astype(F32)
                return earlier[at]

            lax.while_loop(lambda at: at >= 0, more, before)
            put(cell, total[...].astype(BF16))

        return carry

    for g in range(groups):
        loads[g].wait()
        lax.fori_loop(ends[g], ends[g + 1], fill, 0)


def build(src, dst, count, tiles, feats, self_one, neigh_one, bias_one, self_two, neigh_two, bias_two):
    vmem = pl.BlockSpec(memory_space=pltpu.VMEM)
    hbm = pl.BlockSpec(memory_space=pltpu.HBM)
    arrays = [src, dst, tiles, feats, self_one, neigh_one, bias_one, self_two, neigh_two, bias_two]
    arrays = [pltpu.with_memory_space_constraint(array, pltpu.HBM) for array in arrays]
    smem = [pltpu.SMEM((TILES + 8,), jnp.int32)] * 3 + [pltpu.SMEM((264,), jnp.int32)]
    return pl.pallas_call(
        build_kernel,
        out_shape=(
            pltpu.VMEM((32, 256, 512), BF16),
            pltpu.VMEM((32, 512), F32),
            pltpu.VMEM((PACK_ROWS, 256), F32),
        ),
        in_specs=[pl.BlockSpec(memory_space=pltpu.SMEM)] + [hbm] * 10,
        out_specs=(vmem, vmem, vmem),
        scratch_shapes=[
            pltpu.VMEM((TILES, BLK, BLK), BF16),
            pltpu.SMEM((TILES,), jnp.int32),
            pltpu.SMEM((TILES,), jnp.int32),
        ]
        + [pltpu.VMEM(array.shape, array.dtype) for array in arrays[3:]]
        + [pltpu.VMEM((BLK, BLK), F32)]
        + smem
        + [pltpu.SemaphoreType.DMA((TILES // GROUP,)), pltpu.SemaphoreType.DMA((9,))],
        compiler_params=pltpu.CompilerParams(vmem_limit_bytes=12 << 20),
    )(count, *arrays)


def add_up(into, terms):
    rows = into.shape[0]
    step = rows if rows <= 160 else BLK

    def body(i, carry):
        part = pl.ds(pl.multiple_of(i * step, step), step)
        value = terms[0][part, :]
        for term in terms[1:]:
            value = value + term[part, :]
        into[part, :] = value
        return carry

    if rows == step:
        body(0, 0)
    else:
        lax.fori_loop(0, rows // step, body, 0)


class Ring:
    def __init__(self, n, own, extra, land, up_id, down_id, sends, recvs, started):
        self.n, self.middle = n, n // 2
        self.own, self.extra, self.land = own, extra, land
        self.ids = (up_id, down_id)
        self.sends, self.recvs, self.started = sends, recvs, started

    def copy(self, way, distance, half):
        offset = distance if way == 0 else self.n - distance
        slot = (way * self.middle + distance - 1) * 2 + half
        return pltpu.make_async_remote_copy(
            src_ref=self.own(offset, half),
            dst_ref=self.land(way, distance - 1, half),
            send_sem=self.sends.at[slot],
            recv_sem=self.recvs.at[slot],
            device_id=self.ids[way],
            device_id_type=MESH,
        )

    def gather_terms(self, way, distance, half):
        first = self.middle if way == half else self.middle - 1
        if distance == first:
            return []
        self.copy(way, distance + 1, half).wait_recv()
        return [self.land(way, distance, half)]

    def send(self, way, distance, half):
        offset = distance if way == 0 else self.n - distance
        mine = self.own(offset, half)
        terms = [mine] + self.extra(offset, half) + self.gather_terms(way, distance, half)
        if len(terms) > 1:
            add_up(mine, terms)
        copy = self.copy(way, distance, half)
        copy.start()
        self.started.append(copy)

    def early(self, distance):
        self.send(0, distance, 1)
        self.send(1, distance, 0)

    def late(self, distance):
        self.send(0, distance, 0)
        self.send(1, distance, 1)

    def finish(self, half, into=None):
        mine = self.own(0, half)
        terms = [mine] + self.extra(0, half)
        for way in range(2):
            terms += self.gather_terms(way, 0, half)
        add_up(mine if into is None else into, terms)


class Direct:
    def __init__(self, n, own, landing, target_ids, sends, recvs, started):
        self.n, self.own, self.landing, self.ids = n, own, landing, target_ids
        self.sends, self.recvs, self.started = sends, recvs, started

    def copy(self, offset, half):
        slot = (offset - 1) * 2 + half
        return pltpu.make_async_remote_copy(
            src_ref=self.own(offset, half),
            dst_ref=self.landing.at[offset - 1, half],
            send_sem=self.sends.at[slot],
            recv_sem=self.recvs.at[slot],
            device_id=self.ids[offset - 1],
            device_id_type=MESH,
        )

    def send(self, offset):
        for half in range(2):
            copy = self.copy(offset, half)
            copy.start()
            self.started.append(copy)

    def finish(self, half, into):
        terms = [self.own(0, half)]
        for offset in range(1, self.n):
            self.copy(offset, half).wait_recv()
            terms.append(self.landing.at[offset - 1, half])
        add_up(into, terms)


def split(value):
    high = value.astype(BF16)
    rest = value - high.astype(F32)
    middle = rest.astype(BF16)
    low = (rest - middle.astype(F32)).astype(BF16)
    return high, middle, low


def dot(a, b):
    return jnp.dot(a, b, preferred_element_type=F32)


Z_GROUPS = ((0, 96), (96, 32))
X_GROUPS = ((0, 96), (96, 64), (160, 96))
TOGETHER = 2


def reduce_scatter(adj, rhs, bufs, sems, ids, started, after_start, before_end, on_z_rows, on_x_rows):
    sums, sent, got, z_up, z_down, x_up, x_down, tz_up, tz_down, tx_in = bufs
    pair_sends, pair_recvs, sends, recvs = sems
    pair_id, zp_id, zm_id, *x_ids = ids
    xp_id, xm_id = x_ids[0], x_ids[2]
    width = rhs.shape[1]

    def pair_copy(chunk):
        return pltpu.make_async_remote_copy(
            src_ref=sent.at[chunk], dst_ref=got.at[chunk], send_sem=pair_sends.at[chunk],
            recv_sem=pair_recvs.at[chunk], device_id=pair_id, device_id_type=MESH,
        )

    def product(first, target, at):
        lhs = adj[pl.ds(first, TOGETHER)].reshape(TOGETHER * 256, 512)
        target[pl.ds(at, TOGETHER)] = dot(lhs, rhs[...]).reshape(TOGETHER, 256, width)

    def for_pair(i, carry):
        product(16 + i * TOGETHER, sent, i * TOGETHER)
        for k in range(TOGETHER):
            pair_copy(i * TOGETHER + k).start()
        return carry

    def for_own(i, carry):
        product(i * TOGETHER, sums, i * TOGETHER)
        return carry

    def run(kind, first, end):
        lax.fori_loop(first // TOGETHER, end // TOGETHER, kind, 0)

    have = set()

    def arrived(chunk):
        if chunk not in have:
            have.add(chunk)
            pair_copy(chunk).wait_recv()

    def none(offset, half):
        return []

    def z_part(group):
        first, size = Z_GROUPS[group]

        def own(dz, half):
            return sums.at[chunk_z(dz), pl.ds(half * BLK + first, size)]

        def extra(dz, half):
            arrived(chunk_z(dz))
            return [got.at[chunk_z(dz), pl.ds(half * BLK + first, size)]]

        def land(way, at, half):
            return (z_up, z_down)[way].at[at, half, pl.ds(first, size)]

        slots = pl.ds(group * 16, 16)
        return Ring(ZS, own, extra, land, zp_id, zm_id, sends.at[slots], recvs.at[slots], started)

    def x_part(group):
        first, size = X_GROUPS[group]

        def own(dx, half):
            return sums.at[chunk_x(dx, half), pl.ds(first, size)]

        def extra(dx, half):
            arrived(chunk_x(dx, half))
            return [got.at[chunk_x(dx, half), pl.ds(first, size)]]

        def land(way, at, half):
            return (x_up, x_down)[way].at[at, half, pl.ds(first, size)]

        slots = pl.ds(32 + group * 8, 8)
        return Ring(XS, own, extra, land, xp_id, xm_id, sends.at[slots], recvs.at[slots], started)

    def last_z():
        def own(dz, half):
            return sums.at[chunk_x(0, half), pl.ds(rank_of(dz, ZS // 2) * QUARTER, QUARTER)]

        def land(way, at, half):
            return (tz_up, tz_down)[way].at[at, half]

        slots = pl.ds(56, 16)
        return Ring(ZS, own, none, land, zp_id, zm_id, sends.at[slots], recvs.at[slots], started)

    def last_x():
        def own(dx, half):
            return sums.at[chunk_z(0), pl.ds(half * BLK + rank_of(dx, XS // 2) * QUARTER, QUARTER)]

        return Direct(XS, own, tx_in, x_ids, sends.at[pl.ds(72, 6)], recvs.at[pl.ds(72, 6)], started)

    z0, z1, x0, x1, x2, tz, tx = z_part(0), z_part(1), x_part(0), x_part(1), x_part(2), last_z(), last_x()

    run(for_pair, 0, 8)
    run(for_own, 0, 4)
    z0.late(4)
    x0.late(2)
    run(for_pair, 8, 12)
    run(for_own, 4, 8)
    z0.early(3)
    z1.late(4)
    z1.early(3)
    run(for_own, 8, 12)
    x0.early(1)
    run(for_pair, 12, 16)
    run(for_own, 12, 16)
    z0.late(3)
    x0.late(1)
    x1.late(2)
    x1.early(1)
    after_start()
    z0.early(2)
    z1.late(3)
    x0.finish(0)
    x0.finish(1)
    tz.late(4)
    tz.early(3)
    z0.late(2)
    x1.late(1)
    x2.late(2)
    x2.early(1)
    z1.early(2)
    z0.early(1)
    tz.late(3)
    z0.late(1)
    x1.finish(0)
    x1.finish(1)
    tz.early(2)
    z1.late(2)
    x2.late(1)
    z1.early(1)
    tz.late(2)
    z0.finish(0)
    z0.finish(1)
    for dx in (2, 1, 3):
        tx.send(dx)
    z1.late(1)
    before_end()
    x2.finish(0)
    x2.finish(1)
    tz.early(1)
    tz.late(1)
    z1.finish(0)
    z1.finish(1)
    on_z_rows(tx)
    on_x_rows(tz)

    def drain(chunk, carry):
        pair_copy(chunk).wait_send()
        return carry

    return lambda: lax.fori_loop(0, 16, drain, 0)


def net_kernel(adj, feats_ref, pack_ref, out_ref, *scratch):
    (
        feats_all, packs, feats, hidden, self_one, neigh_one, self_two, neigh_two, bias, own_part, agg_all, agg_two, slices,
        landed, *rest
    ) = scratch
    bufs_one, bufs_two, rest = rest[:10], rest[10:20], rest[20:]
    y_sends, y_recvs, sems_one, sems_two = rest[0], rest[1], rest[2:6], rest[6:10]

    feat = lax.axis_index("feat")
    x, z, core = position()

    def at(x_at, z_at, core_at, feat_at=feat):
        return feat_at, (x_at * ZS + z_at) * 2 + core_at

    pair_id = at(x, z, 1 - core)
    zp_id, zm_id = at(x, lax.rem(z + 1, ZS), core), at(x, lax.rem(z + ZS - 1, ZS), core)
    x_ids = [at(lax.rem(x + k, XS), z, core) for k in range(1, XS)]
    y_ids = [at(x, z, core, lax.rem(feat + k, FS)) for k in range(1, FS)]
    ids = (pair_id, zp_id, zm_id, *x_ids)

    barrier = pltpu.get_barrier_semaphore()
    for other in ids + tuple(y_ids):
        pl.semaphore_signal(barrier, inc=1, device_id=other, device_id_type=MESH)
    pl.semaphore_wait(barrier, 9)

    started = []

    def to_y(kind, source, target):
        copies = []
        for k in range(1, FS):
            slot = kind * 3 + k - 1
            copies.append(
                pltpu.make_async_remote_copy(
                    src_ref=source(k), dst_ref=target, send_sem=y_sends.at[slot], recv_sem=y_recvs.at[slot],
                    device_id=y_ids[k - 1], device_id_type=MESH,
                )
            )
            copies[-1].start()
        if kind != 4:
            started.extend(copies)
        return copies

    def received(copies):
        for copy in copies:
            copy.wait_recv()

    feats_rows = pl.ds(pl.multiple_of(feat * 32, 32), 32)
    feats_copies = to_y(0, lambda k: feats_ref, feats_all.at[feats_rows])
    feats_all[feats_rows, :] = feats_ref[...]
    packs[feat] = pack_ref[...]
    received(feats_copies)
    feats[...] = feats_all[...].T.astype(BF16)

    pack_copies = []

    def send_pack(kind, first, size):
        rows = pl.ds(first, size)
        pack_copies.append(to_y(kind, lambda k: pack_ref.at[rows], packs.at[feat, rows]))

    def take_weights():
        received(pack_copies[0])
        low = lax.broadcasted_iota(jnp.int32, (1, BLK), 1) < 64
        for row in range(2):
            for pair in range(2):
                left = packs[2 * pair, 64 + row : 65 + row, 0:BLK]
                right = packs[2 * pair + 1, 64 + row : 65 + row, 0:BLK]
                value = jnp.where(low, left, pltpu.roll(right, 64, 1))
                bias[row : row + 1, pair * BLK : (pair + 1) * BLK] = value
        for j in range(FS):
            self_one[32 * j : 32 * (j + 1), :] = packs[j, 0:32, :].astype(BF16)
            neigh_one[32 * j : 32 * (j + 1), :] = packs[j, 32:64, :].astype(BF16)

        own_part[...] = dot(feats[...], self_one[...]) + bias[0:1, :]

    own = pl.ds(pl.multiple_of(feat * BLK, BLK), BLK)

    def own_of_two():
        received(pack_copies[1])
        for j in range(FS):
            self_two[64 * j : 64 * (j + 1), :] = packs[j, 72:136, :].astype(BF16)
            neigh_two[64 * j : 64 * (j + 1), :] = packs[j, 136:200, :].astype(BF16)
        own_part[0:BLK, :] = dot(hidden[own, :], self_two[...]) + bias[1:2, :]

    agg_copies = []

    def share(kind, rows, ring):
        for half in range(2):
            ring.finish(half, agg_all.at[feat, pl.ds(rows + half * QUARTER, QUARTER)])
        part = agg_all.at[feat, pl.ds(rows, 64)]
        agg_copies.extend(to_y(kind, lambda k: part, part))

    drain_one = reduce_scatter(
        adj, feats, bufs_one, sems_one, ids, started, lambda: send_pack(1, 0, 72), take_weights,
        lambda ring: share(2, 64, ring), lambda ring: share(3, 0, ring),
    )
    received(agg_copies)

    pre = own_part[...]
    for part in split(agg_all[...].reshape(FS * BLK, BLK)):
        pre = pre + dot(part, neigh_one[...])
    hidden[...] = jnp.maximum(pre, 0.0).astype(BF16)

    def keep(rows, ring):
        for half in range(2):
            ring.finish(half, agg_two.at[pl.ds(rows + half * QUARTER, QUARTER)])

    drain_two = reduce_scatter(
        adj, hidden, bufs_two, sems_two, ids, started, lambda: send_pack(5, 72, 128), own_of_two,
        lambda ring: keep(64, ring), lambda ring: keep(0, ring),
    )

    pre = own_part[0:BLK, :]
    for part in split(agg_two[...]):
        pre = pre + dot(part, neigh_two[...])
    result = jnp.maximum(pre, 0.0)
    slices[...] = result.T.reshape(FS, 64, BLK)
    out_copies = to_y(4, lambda k: slices.at[lax.rem(feat + k, FS)], landed.at[feat])
    landed[feat] = slices[feat]
    drain_one()
    drain_two()
    for copy in started:
        copy.wait_send()
    received(out_copies)
    for j in range(FS):
        out_ref[:, j * BLK : (j + 1) * BLK] = landed[j].astype(BF16)

    for copy in out_copies:
        copy.wait_send()


def layer_buffers(width):
    shapes = [(16, 256, width)] * 3
    shapes += [(4, 2, 128, width)] * 2 + [(2, 2, 256, width)] * 2 + [(4, 2, 32, width)] * 2 + [(3, 2, 32, width)]
    return [pltpu.VMEM(shape, F32) for shape in shapes]


def net(adj, feats, pack):
    vmem = pl.BlockSpec(memory_space=pltpu.VMEM)
    dma = pltpu.SemaphoreType.DMA
    return pl.pallas_call(
        net_kernel,
        out_shape=jax.ShapeDtypeStruct((64, 512), BF16),
        in_specs=[vmem] * 3,
        out_specs=vmem,
        scratch_shapes=[
            pltpu.VMEM((128, 512), F32),
            pltpu.VMEM((FS, PACK_ROWS, 256), F32),
            pltpu.VMEM((512, 128), BF16),
            pltpu.VMEM((512, 256), BF16),
            pltpu.VMEM((128, 256), BF16),
            pltpu.VMEM((128, 256), BF16),
            pltpu.VMEM((256, 256), BF16),
            pltpu.VMEM((256, 256), BF16),
            pltpu.VMEM((8, 256), F32),
            pltpu.VMEM((512, 256), F32),
            pltpu.VMEM((FS, 128, 128), F32),
            pltpu.VMEM((128, 256), F32),
            pltpu.VMEM((FS, 64, 128), F32),
            pltpu.VMEM((FS, 64, 128), F32),
        ]
        + layer_buffers(128)
        + layer_buffers(256)
        + [dma((18,)), dma((18,))]
        + [dma((16,)), dma((16,)), dma((80,)), dma((80,))] * 2,
        compiler_params=pltpu.CompilerParams(
            collective_id=0, has_side_effects=True, vmem_limit_bytes=36 << 20
        ),
    )(*[pltpu.with_memory_space_constraint(array, pltpu.VMEM) for array in (adj, feats, pack)])


def on_device(
    feats, tile_src, tile_dst, tile_val, tile_count, self_one, neigh_one, bias_one, self_two, neigh_two, bias_two
):
    adj, columns, pack = build(
        tile_src, tile_dst, tile_count, tile_val, feats.T, self_one, neigh_one, bias_one.reshape(1, 64), self_two,
        neigh_two, bias_two.reshape(1, 64),
    )
    return net(adj, columns, pack).T


def solution(mesh):
    placed = (
        P("dom", "feat"),
        P("dom"),
        P("dom"),
        P("dom", None, None),
        P("dom"),
        P("feat", None),
        P("feat", None),
        P("feat"),
        P("feat", None),
        P("feat", None),
        P("feat"),
    )
    return jax.shard_map(
        on_device, mesh=mesh, in_specs=placed, out_specs=P("dom", "feat"), check_vma=False
    )
```
